256 devices in a mesh: seq: 64 (over x, z, core), tp: 4 (over y).
Axes of the slice: x: 4, y: 4, z: 8, core: 2. Of those that a mesh axis runs over, the one named last changes fastest.
Arguments:
- hidden_in: bfloat16 [256, 2048], P('seq'), may hold values from -6 to 6
- query_weight: bfloat16 [2048, 2048], P(None, 'tp'), may hold values from -0.125 to 0.125
- key_weight: bfloat16 [2048, 2048], P(None, 'tp'), may hold values from -0.125 to 0.125
- value_weight: bfloat16 [2048, 2048], P(None, 'tp'), may hold values from -0.125 to 0.125
- out_weight: bfloat16 [2048, 2048], P('tp'), may hold values from -0.125 to 0.125
- query_gain: float32 [2048], P('tp'), may hold values from 0.5 to 1.5
- key_gain: float32 [2048], P('tp'), may hold values from 0.5 to 1.5
- post_gain: float32 [2048], P('tp'), may hold values from 0.5 to 1.5
- key_cache: bfloat16 [4, 8192, 2048], P(None, 'seq', 'tp'), may hold values from -110 to 110
- value_cache: bfloat16 [4, 8192, 2048], P(None, 'seq', 'tp'), may hold values from -6 to 6
- cache_lengths: int32 [4], replicated, may hold values from 1024 to 8128
- parents: int32 [4, 64], replicated, may hold values from -1 to 62, as said below
- accepted_leaf: int32 [4], replicated, may hold values from 0 to 63
Outputs:
- hidden_out: bfloat16 [256, 2048], P('seq', 'tp')
- new_key_cache: bfloat16 [4, 8192, 2048], P(None, 'seq', 'tp')
- new_value_cache: bfloat16 [4, 8192, 2048], P(None, 'seq', 'tp')
The draws below stay inside these ranges and needn't reach their ends.
Inputs may be any that keep to these rules, and one draw needn't show every extreme that they name: parents[r, 0] = -1; for i >= 1, parents[r, i] lies in max(0, i - 3) to i - 1; parents[r, 63] = 62.
All inputs are finite; a program needn't handle non-finite values.
Results may differ from the reference program's by a relative error of at most 0.019.
Values may be sent and summed in bfloat16 or wider, within the bound.
A program may use at most 128 MiB of HBM per device.

```python
import math
import jax
import jax.numpy as jnp
from jax import lax

D = 2048
HEADS = 16
HEAD_DIM = 128
REQ = 4
DRAFT = 64
QDIM = 2048
TOKENS = 256
CACHE_TOTAL = 8192


def draw_key_cache(key, part):
    normal_part = jnp.clip(jax.random.normal(jax.random.fold_in(key, 3), (REQ, CACHE_TOTAL, QDIM), jnp.float32), -5.0, 5.0)
    return normal_part.astype(jnp.bfloat16)


def draw_cache_lengths(key, part):
    lowest = CACHE_TOTAL // 8
    highest = CACHE_TOTAL - DRAFT
    lengths_drawn = jax.random.randint(jax.random.fold_in(key, 1), (REQ,), lowest, highest + 1)
    chosen = jax.random.randint(jax.random.fold_in(key, 2), (), 0, REQ)
    return jnp.where(jnp.arange(REQ) == chosen, highest, lengths_drawn).astype(jnp.int32)


def draw_parents(key, part):
    indices = jnp.arange(DRAFT, dtype=jnp.int32)[None, :]
    backward = jax.random.randint(jax.random.fold_in(key, 6), (REQ, DRAFT), 0, 3)
    parent_ids = indices - 1 - jnp.minimum(backward, jnp.maximum(indices - 1, 0))
    parent_ids = jnp.where(indices == DRAFT - 1, DRAFT - 2, parent_ids)
    return parent_ids.astype(jnp.int32)


def place_ends(result, own_key, low, high):
    longest = result.shape.index(max(result.shape))
    spots = []
    for shift in (0, 1):
        where = [jax.random.randint(jax.random.fold_in(own_key, axis), (), 0, length) for axis, length in enumerate(result.shape)]
        where[longest] = (where[longest] + shift) % result.shape[longest]
        spots.append(tuple(where))
    return result.at[spots[0]].set(low).at[spots[1]].set(high)


def level_of(rng, extent, shards, least, largest):
    factor_of, own = 1.0, jax.random.fold_in(rng, 6)
    for axis_at, shards_of in shards:
        steps = jnp.exp(jax.random.uniform(jax.random.fold_in(own, axis_at), (shards_of,), jnp.float32, least / len(shards), largest / len(shards)))
        factor_of = factor_of * jnp.repeat(steps, extent[axis_at] // shards_of).reshape([-1 if axis == axis_at else 1 for axis in range(len(extent))])
    return factor_of


def bell_draw(rng, shape, width, most, split=(), kind=jnp.bfloat16):
    factor_of = level_of(rng, shape, split, -0.22, 0.18) if split else 1.0
    values = jax.random.normal(rng, shape, jnp.float32) * width * factor_of
    return jnp.minimum(jnp.maximum(values, -most), most).astype(kind)


def setup_inputs(seed: int = 0) -> dict:
    arg_keys = jax.random.split(jax.random.key(seed), 14)
    hidden_in = bell_draw(arg_keys[0], (TOKENS, D), 1.0, 6.0, ((0, 64),))
    query_weight = bell_draw(arg_keys[1], (D, QDIM), D ** -0.5, 0.125, ((1, 4),))
    key_weight = bell_draw(arg_keys[2], (D, QDIM), D ** -0.5, 0.125, ((1, 4),))
    value_weight = bell_draw(arg_keys[3], (D, QDIM), D ** -0.5, 0.125, ((1, 4),))
    out_weight = bell_draw(arg_keys[4], (QDIM, D), QDIM ** -0.5, 0.125, ((0, 4),))
    query_gain = jnp.clip(0.5 + 1.0 * jax.random.uniform(arg_keys[5], (QDIM,), jnp.float32) ** level_of(arg_keys[5], (QDIM,), ((0, 4),), -0.2, 0.2), 0.5, 1.5)
    key_gain = jnp.clip(0.5 + 1.0 * jax.random.uniform(arg_keys[6], (QDIM,), jnp.float32) ** level_of(arg_keys[6], (QDIM,), ((0, 4),), -0.2, 0.2), 0.5, 1.5)
    post_gain = jnp.clip(0.5 + 1.0 * jax.random.uniform(arg_keys[7], (D,), jnp.float32) ** level_of(arg_keys[7], (D,), ((0, 4),), -0.2, 0.2), 0.5, 1.5)
    key_cache = draw_key_cache(jax.random.fold_in(arg_keys[13], 71), 0)
    value_cache = bell_draw(arg_keys[9], (REQ, CACHE_TOTAL, QDIM), 1.0, 6.0, ((1, 64), (2, 4)))
    cache_lengths = draw_cache_lengths(jax.random.fold_in(arg_keys[13], 71), 0)
    parents = draw_parents(jax.random.fold_in(arg_keys[13], 71), 0)
    accepted_leaf = place_ends(jax.random.randint(arg_keys[12], (REQ,), 0, DRAFT), jax.random.fold_in(arg_keys[12], 1), 0, DRAFT - 1).astype(jnp.int32)
    return {"hidden_in": hidden_in, "query_weight": query_weight, "key_weight": key_weight, "value_weight": value_weight, "out_weight": out_weight, "query_gain": query_gain, "key_gain": key_gain, "post_gain": post_gain, "key_cache": key_cache, "value_cache": value_cache, "cache_lengths": cache_lengths, "parents": parents, "accepted_leaf": accepted_leaf}


EPS = 1e-06
THETA = 500000.0
NEG = -1e+30

def ancestry(parents):
    number = parents.shape[-1]
    columns = jnp.arange(number, dtype=jnp.int32)
    single = (parents[:, :, None] == columns[None, None, :]).astype(jnp.float32)
    ancestors = jnp.eye(number, dtype=jnp.float32)[None] + single
    for repeat in range(max(1, (number - 1).bit_length())):
        ancestors = jnp.minimum(jnp.einsum('rij,rjk->rik', ancestors, ancestors, precision=lax.Precision.HIGHEST), 1.0)
    tree_depth = lax.optimization_barrier(jnp.sum(ancestors, axis=-1)) - 1.0
    return (ancestors, tree_depth)

def rotary(values, positions):
    half_dim = values.shape[-1] // 2
    freqs = THETA ** (-2.0 * jnp.arange(half_dim, dtype=jnp.float32) / values.shape[-1])
    angles = positions[:, None, None] * freqs[None, None, :]
    cosine = jnp.cos(angles)
    sine = jnp.sin(angles)
    first = values[..., :half_dim]
    second = values[..., half_dim:]
    return jnp.concatenate([first * cosine - second * sine, second * cosine + first * sine], axis=-1)

def prepare(raw, square_sum, gain, positions, width_all):
    scaled = raw * lax.rsqrt(square_sum / width_all + EPS)[:, None] * gain[None, :]
    rows_here = raw.shape[0]
    heads_here = raw.shape[1] // HEAD_DIM
    turned = rotary(scaled.reshape(rows_here, heads_here, HEAD_DIM), positions)
    return turned.reshape(rows_here, heads_here * HEAD_DIM).astype(jnp.bfloat16)

def reference(hidden_in, query_weight, key_weight, value_weight, out_weight, query_gain, key_gain, post_gain, key_cache, value_cache, cache_lengths, parents, accepted_leaf):
    ancestors, tree_depth = ancestry(parents)
    positions = (cache_lengths[:, None].astype(jnp.float32) + tree_depth).reshape(TOKENS)
    query_raw = jnp.dot(hidden_in, query_weight, preferred_element_type=jnp.float32)
    key_raw = jnp.dot(hidden_in, key_weight, preferred_element_type=jnp.float32)
    value_raw = jnp.dot(hidden_in, value_weight, preferred_element_type=jnp.float32)
    queries = prepare(query_raw, lax.optimization_barrier(jnp.sum(query_raw * query_raw, axis=1)), query_gain, positions, QDIM)
    keys = prepare(key_raw, lax.optimization_barrier(jnp.sum(key_raw * key_raw, axis=1)), key_gain, positions, QDIM)
    values = value_raw.astype(jnp.bfloat16)
    factor = 1.0 / math.sqrt(HEAD_DIM)
    places = jnp.arange(CACHE_TOTAL, dtype=jnp.int32)
    query_blocks = queries.reshape(REQ, DRAFT, HEADS, HEAD_DIM)
    key_blocks = keys.reshape(REQ, DRAFT, HEADS, HEAD_DIM)
    value_blocks = values.reshape(REQ, DRAFT, HEADS, HEAD_DIM)
    cache_keys = key_cache.reshape(REQ, CACHE_TOTAL, HEADS, HEAD_DIM)
    cache_values = value_cache.reshape(REQ, CACHE_TOTAL, HEADS, HEAD_DIM)

    def attend(item):
        query_block, key_block, value_block, stored_keys, stored_values, length, tree = item
        query_float = query_block.astype(jnp.float32)
        cache_scores = jnp.einsum('ihd,lhd->ihl', query_float, stored_keys.astype(jnp.float32), precision=lax.Precision.HIGHEST) * factor
        visible = (places < length)[None, None, :]
        cache_scores = jnp.where(visible, cache_scores, NEG)
        draft_scores = jnp.einsum('ihd,jhd->ihj', query_float, key_block.astype(jnp.float32), precision=lax.Precision.HIGHEST) * factor
        tree_mask = (tree > 0.5)[:, None, :]
        draft_scores = jnp.where(tree_mask, draft_scores, NEG)
        highest = jnp.maximum(lax.optimization_barrier(jnp.max(cache_scores, axis=-1)), lax.optimization_barrier(jnp.max(draft_scores, axis=-1)))
        cache_weights = jnp.where(visible, jnp.exp(cache_scores - highest[..., None]), 0.0)
        draft_weights = jnp.where(tree_mask, jnp.exp(draft_scores - highest[..., None]), 0.0)
        denominator = lax.optimization_barrier(jnp.sum(cache_weights, axis=-1)) + lax.optimization_barrier(jnp.sum(draft_weights, axis=-1))
        summed = jnp.einsum('ihl,lhd->ihd', cache_weights, stored_values.astype(jnp.float32), precision=lax.Precision.HIGHEST)
        summed = summed + jnp.einsum('ihj,jhd->ihd', draft_weights, value_block.astype(jnp.float32), precision=lax.Precision.HIGHEST)
        return (summed / denominator[..., None]).reshape(DRAFT, QDIM).astype(jnp.bfloat16)
    attention = lax.map(attend, (query_blocks, key_blocks, value_blocks, cache_keys, cache_values, cache_lengths, ancestors)).reshape(TOKENS, QDIM)
    projected = jnp.dot(attention, out_weight, preferred_element_type=jnp.float32)
    power = lax.optimization_barrier(jnp.sum(projected * projected, axis=1)) / D
    normed = projected * lax.rsqrt(power + EPS)[:, None] * post_gain[None, :]
    hidden_out = (hidden_in.astype(jnp.float32) + normed).astype(jnp.bfloat16)

    def compact(item):
        stored_keys, stored_values, key_block, value_block, length, tree, leaf, levels = item
        on_path = tree[leaf]
        target = length + levels.astype(jnp.int32)
        placing = (places[:, None] == target[None, :]) & (on_path[None, :] > 0.5)
        written = jnp.any(placing, axis=-1)[:, None]
        placing_half = placing.astype(jnp.bfloat16)
        fresh_keys = jnp.dot(placing_half, key_block, preferred_element_type=jnp.float32).astype(jnp.bfloat16)
        fresh_values = jnp.dot(placing_half, value_block, preferred_element_type=jnp.float32).astype(jnp.bfloat16)
        return (jnp.where(written, fresh_keys, stored_keys), jnp.where(written, fresh_values, stored_values))
    new_key_cache, new_value_cache = lax.map(compact, (key_cache, value_cache, keys.reshape(REQ, DRAFT, QDIM), values.reshape(REQ, DRAFT, QDIM), cache_lengths, ancestors, accepted_leaf, tree_depth))
    return (hidden_out, new_key_cache, new_value_cache)
```

```python
import math

import jax
import jax.numpy as jnp
import numpy as np
from jax import lax
from jax.experimental import pallas as pl
from jax.experimental.pallas import tpu as pltpu
from jax.sharding import PartitionSpec as P

HEAD_DIM = 128
EPS = 1e-06
THETA = 500000.0
NEG = -1e30
NX, NZ, NC, NT = 4, 8, 2, 4
HEADS = 4
OWN = 4
ROWS = HEADS * OWN
DRAFT = 64
REQ = 4
WIDTH = HEADS * HEAD_DIM
BLOCK = 128
MESH = pl.DeviceIdType.MESH
F32 = jnp.float32
BF16 = jnp.bfloat16
PLANES = (0, 1, 3, 2)
FAR_Z = (4, 3, 5, 2, 6, 1, 7, 0)


def far_first():
    hops = lambda a, b: min(a, NX - a) + min(b, NZ - b)
    pairs = [(a, b) for a in range(NX) for b in range(NZ) if (a, b) != (0, 0)]
    return sorted(pairs, key=lambda pair: -hops(*pair))


def iota(shape, dim):
    return lax.broadcasted_iota(jnp.int32, shape, dim)


def nt_dot(a, b):
    return lax.dot_general(a, b, (((1,), (1,)), ((), ())), preferred_element_type=F32)


def dot(a, b):
    return jnp.dot(a, b, preferred_element_type=F32)


def kernel(
    hid, wq, wk, wv, wo, qg, kg, pg, kc, vc, lens, par, leaf, freq,
    out_h, out_k, out_v,
    hid_s, wq_s, wk_s, wv_s, wo_s, qg_s, kg_s, pg_s, par_s, freq_s, lens_s, leaf_s,
    kfull, vfull, anc_s, sq_send, sq_recv, q_own, k_own, v_own, qbuf, kbuf, vbuf,
    o_st, s_st, obuf, sbuf, att_s, pr_s, pr_send, pr_recv, nk_s, nv_s, oh_s,
    lsem, swap_sem, sq_sem, q_sem, q_send, z_sem, x_sem, c_sem, o_sem, s_sem, p_sem, out_sem,
):
    seq = lax.axis_index("seq")
    tp = lax.axis_index("tp")
    core = lax.rem(seq, NC)
    zz = lax.rem(seq // NC, NZ)
    xx = seq // (NC * NZ)

    def at(dx, dz):
        return ((lax.rem(xx + dx, NX) * NZ + lax.rem(zz + dz, NZ)) * NC + core, tp)

    partner = (seq + 1 - 2 * core, tp)
    y_peers = [(seq, lax.rem(tp + d, NT)) for d in range(1, NT)]
    plane_peers = [at(a, b) for a, b in far_first()]

    barrier = pltpu.get_barrier_semaphore()
    for peer in plane_peers + y_peers + [partner]:
        pl.semaphore_signal(barrier, inc=1, device_id=peer, device_id_type=MESH)

    pairs = [
        (par, par_s), (lens, lens_s), (freq, freq_s), (hid, hid_s), (wq, wq_s), (wk, wk_s), (wv, wv_s),
        (qg, qg_s), (kg, kg_s), (pg, pg_s), (leaf, leaf_s),
        (kc, kfull.at[:, pl.ds(core * BLOCK, BLOCK), :]),
        (vc, vfull.at[:, pl.ds(core * BLOCK, BLOCK), :]),
        (wo, wo_s),
    ]
    local = [pltpu.make_async_copy(a, b, lsem.at[i]) for i, (a, b) in enumerate(pairs)]
    for copy in local:
        copy.start()
    (c_par, c_lens, c_freq, c_hid, c_wq, c_wk, c_wv, c_qg, c_kg, c_pg, c_leaf, c_kc, c_vc, c_wo) = local

    def remote(src, dst, send, recv, peer):
        copy = pltpu.make_async_remote_copy(
            src_ref=src, dst_ref=dst, send_sem=send, recv_sem=recv, device_id=peer, device_id_type=MESH
        )
        copy.start()

    def wait(ref, sem):
        pltpu.make_async_copy(ref, ref, sem).wait()

    c_par.wait()
    square = (DRAFT, DRAFT)
    eye = (iota(square, 0) == iota(square, 1)).astype(F32)
    chains = []
    for r in range(REQ):
        up = (par_s[pl.ds(r, 1), :] == iota(square, 0)).astype(F32)
        chains.append((eye + up).astype(BF16))
    for _ in range(6):
        chains = [jnp.minimum(dot(a, a), 1.0).astype(BF16) for a in chains]
    for r in range(REQ):
        anc_s[r] = chains[r]

    chunk = (ROWS, HEAD_DIM)
    row_head = (iota(chunk, 0) >> 2) & 3
    lane = iota(chunk, 1)
    row_token = (zz * NC + core) * OWN + (iota((ROWS, DRAFT), 0) & 3)
    one_hot = (iota((ROWS, DRAFT), 1) == row_token).astype(F32).astype(BF16)
    anc_rows = nt_dot(one_hot, anc_s[xx])
    depth = jnp.sum(anc_rows, axis=1, keepdims=True) - 1.0
    c_lens.wait()
    position = lens_s[xx].astype(F32) + depth
    c_freq.wait()
    angle = position * freq_s[...]
    cosine = jnp.cos(angle)
    sine = jnp.sin(angle)
    sine = jnp.where(lane < HEAD_DIM // 2, -sine, sine)

    c_hid.wait()
    h4 = hid_s[...].astype(F32)
    h8 = jnp.concatenate([h4, h4], axis=0)
    h16 = jnp.concatenate([h8, h8], axis=0).astype(BF16)

    def diagonal(wide):
        picked = wide[:, :HEAD_DIM]
        for h in range(1, HEADS):
            picked = jnp.where(row_head == h, wide[:, h * HEAD_DIM : (h + 1) * HEAD_DIM], picked)
        return picked

    def spread(gain):
        return diagonal(jnp.broadcast_to(gain, (ROWS, WIDTH)))

    c_wq.wait()
    q_wide = dot(h16, wq_s[...])
    c_wk.wait()
    k_wide = dot(h16, wk_s[...])
    q_sq = jnp.sum(q_wide * q_wide, axis=1, keepdims=True)
    k_sq = jnp.sum(k_wide * k_wide, axis=1, keepdims=True)
    lane8 = iota((8, HEAD_DIM), 1)
    sq_mine = jnp.where(lane8 < HEAD_DIM // 2, q_sq[:8], k_sq[:8])
    sq_send[...] = sq_mine
    c_wv.wait()
    v_own[...] = diagonal(dot(h16, wv_s[...])).astype(BF16)
    for copy in (c_qg, c_kg):
        copy.wait()
    q_turn = diagonal(q_wide) * spread(qg_s[...])
    k_turn = diagonal(k_wide) * spread(kg_s[...])
    q_turn = q_turn * cosine + pltpu.roll(q_turn, HEAD_DIM // 2, 1) * sine
    k_turn = k_turn * cosine + pltpu.roll(k_turn, HEAD_DIM // 2, 1) * sine

    pl.semaphore_wait(barrier, len(plane_peers) + len(y_peers) + 1)

    for i, peer in enumerate(y_peers):
        remote(sq_send, sq_recv.at[i], sq_sem.at[0], sq_sem.at[1], peer)
    mine = pl.ds(core * BLOCK, BLOCK)
    remote(kc, kfull.at[:, mine, :], swap_sem.at[0], swap_sem.at[1], partner)
    remote(vc, vfull.at[:, mine, :], swap_sem.at[2], swap_sem.at[3], partner)

    wait(sq_recv, sq_sem.at[1])
    total = sq_mine + sq_recv[0] + sq_recv[1] + sq_recv[2]
    scale = lax.rsqrt(total / (NT * WIDTH) + EPS)
    other = pltpu.roll(scale, HEAD_DIM // 2, 1)
    q_scale = jnp.where(lane8 < HEAD_DIM // 2, scale, other)
    k_scale = jnp.where(lane8 < HEAD_DIM // 2, other, scale)
    q_own[...] = (q_turn * jnp.concatenate([q_scale, q_scale], axis=0)).astype(BF16)
    k_own[...] = (k_turn * jnp.concatenate([k_scale, k_scale], axis=0)).astype(BF16)

    for peer in plane_peers:
        remote(q_own, qbuf.at[xx * NZ + zz], q_send, q_sem.at[xx], peer)
    pltpu.make_async_copy(q_own, qbuf.at[xx * NZ + zz], q_sem.at[xx]).start()
    for dz in FAR_Z[:-1]:
        remote(k_own, kbuf.at[core, xx, zz], z_sem.at[0], z_sem.at[1], at(0, dz))
        remote(v_own, vbuf.at[core, xx, zz], z_sem.at[2], z_sem.at[3], at(0, dz))
    pltpu.make_async_copy(k_own, kbuf.at[core, xx, zz], z_sem.at[1]).start()
    pltpu.make_async_copy(v_own, vbuf.at[core, xx, zz], z_sem.at[3]).start()

    factor = 1.0 / math.sqrt(HEAD_DIM)
    tall = (NZ * ROWS, NC * BLOCK)
    tall_head = (iota(tall, 0) >> 2) & 3
    place = (seq - core) * BLOCK + iota(tall, 1)
    turn = iota((NZ * ROWS, HEAD_DIM), 0) == iota((NZ * ROWS, HEAD_DIM), 1)
    c_kc.wait()
    c_vc.wait()
    wait(kfull.at[:, mine, :], swap_sem.at[1])
    wait(vfull.at[:, mine, :], swap_sem.at[3])
    for step, dx in enumerate(PLANES):
        r = lax.rem(xx + dx, NX)
        group = pl.ds(r * NZ, NZ)
        wait(qbuf.at[group], q_sem.at[r])
        queries = qbuf[group].reshape(NZ * ROWS, HEAD_DIM)
        scores = None
        for h in range(HEADS):
            part = nt_dot(queries, kfull[r, :, h * HEAD_DIM : (h + 1) * HEAD_DIM])
            scores = part if h == 0 else jnp.where(tall_head == h, part, scores)
        visible = place < lens_s[r]
        scores = jnp.where(visible, scores * factor, NEG)
        peak = jnp.max(scores, axis=1, keepdims=True)
        weights = jnp.where(visible, jnp.exp(scores - peak), 0.0)
        weight_sum = jnp.sum(weights, axis=1, keepdims=True)
        mixed = None
        for h in range(HEADS):
            masked = jnp.where(tall_head == h, weights, 0.0).astype(BF16)
            part = dot(masked, vfull[r, :, h * HEAD_DIM : (h + 1) * HEAD_DIM])
            mixed = part if h == 0 else mixed + part
        o_st[step] = mixed.astype(BF16).reshape(NZ, ROWS, HEAD_DIM)
        s_st[step, :, :HEAD_DIM] = jnp.sum(jnp.where(turn, peak, 0.0), axis=0, keepdims=True)
        s_st[step, :, HEAD_DIM:] = jnp.sum(jnp.where(turn, weight_sum, 0.0), axis=0, keepdims=True)
        slot = xx * NZ + zz
        for dz in FAR_Z:
            to = lax.rem(zz + dz, NZ)
            if (dx, dz) == (0, 0):
                pltpu.make_async_copy(o_st.at[step, to], obuf.at[slot], o_sem.at[1]).start()
                pltpu.make_async_copy(s_st.at[step], sbuf.at[slot], s_sem.at[1]).start()
            else:
                remote(s_st.at[step], sbuf.at[slot], s_sem.at[0], s_sem.at[1], at(dx, dz))
                remote(o_st.at[step, to], obuf.at[slot], o_sem.at[0], o_sem.at[1], at(dx, dz))

    wait(kbuf.at[core, xx], z_sem.at[1])
    wait(vbuf.at[core, xx], z_sem.at[3])
    remote(kbuf.at[core, xx], kbuf.at[core, xx], c_sem.at[0], c_sem.at[1], partner)
    remote(vbuf.at[core, xx], vbuf.at[core, xx], c_sem.at[2], c_sem.at[3], partner)
    for dx in (2, 1, 3):
        remote(kbuf.at[core, xx], kbuf.at[core, xx], x_sem.at[0], x_sem.at[1 + dx], at(dx, 0))
        remote(vbuf.at[core, xx], vbuf.at[core, xx], x_sem.at[1], x_sem.at[4 + dx], at(dx, 0))

    wait(kbuf.at[core, xx], c_sem.at[1])
    wait(vbuf.at[core, xx], c_sem.at[3])
    both = NC * NZ * ROWS
    col = iota((DRAFT, both), 1)
    col_token = ((col >> 4) & 7) * (NC * OWN) + (col >> 7) * OWN + (col & 3)
    expand = (iota((DRAFT, both), 0) == col_token).astype(F32).astype(BF16)
    allowed = dot(anc_rows.astype(BF16), expand) > 0.5
    wide_shape = (ROWS, both)
    allowed = allowed & (((iota(wide_shape, 1) >> 2) & 3) == ((iota(wide_shape, 0) >> 2) & 3))

    def request_rows(buf, r):
        return jnp.concatenate([buf[c, r].reshape(NZ * ROWS, HEAD_DIM) for c in range(NC)], axis=0)

    d_scores = jnp.where(allowed, nt_dot(q_own[...], request_rows(kbuf, xx)) * factor, NEG)
    d_peak = jnp.max(d_scores, axis=1, keepdims=True)
    d_weights = jnp.where(allowed, jnp.exp(d_scores - d_peak), 0.0)
    d_sum = jnp.sum(d_weights, axis=1, keepdims=True)
    d_out = dot(d_weights.astype(BF16), request_rows(vbuf, xx))

    for i, dx in enumerate((1, 3, 2)):
        r = lax.rem(xx + dx, NX)
        wait(kbuf.at[core, r], x_sem.at[1 + (NX - dx)])
        wait(vbuf.at[core, r], x_sem.at[4 + (NX - dx)])
        remote(kbuf.at[core, r], kbuf.at[core, r], c_sem.at[4 + 4 * i], c_sem.at[5 + 4 * i], partner)
        remote(vbuf.at[core, r], vbuf.at[core, r], c_sem.at[6 + 4 * i], c_sem.at[7 + 4 * i], partner)

    c_leaf.wait()
    p_place = (seq * BLOCK + iota((BLOCK, DRAFT), 0)).astype(F32)
    col_head = (iota((BLOCK, both), 1) >> 2) & 3
    for i, dx in enumerate((0, 1, 3, 2)):
        r = lax.rem(xx + dx, NX)
        if dx:
            wait(kbuf.at[core, r], c_sem.at[1 + 4 * i])
            wait(vbuf.at[core, r], c_sem.at[3 + 4 * i])
        anc = anc_s[r]
        target = jnp.sum(anc.astype(F32), axis=0, keepdims=True) - 1.0 + lens_s[r].astype(F32)
        leaf_hot = (iota((ROWS, DRAFT), 1) == leaf_s[r]).astype(F32).astype(BF16)
        on_path = nt_dot(leaf_hot, anc)[:1]
        placing = jnp.where((p_place == target) & (on_path > 0.5), 1.0, 0.0)
        written = jnp.sum(placing, axis=1, keepdims=True) > 0.5
        placing = dot(placing.astype(BF16), expand)
        k_rows = request_rows(kbuf, r)
        v_rows = request_rows(vbuf, r)
        for h in range(HEADS):
            columns = slice(h * HEAD_DIM, (h + 1) * HEAD_DIM)
            pick = jnp.where(col_head == h, placing, 0.0).astype(BF16)
            old_k = kfull[r, mine, columns].astype(F32)
            old_v = vfull[r, mine, columns].astype(F32)
            nk_s[r, :, columns] = jnp.where(written, dot(pick, k_rows), old_k).astype(BF16)
            nv_s[r, :, columns] = jnp.where(written, dot(pick, v_rows), old_v).astype(BF16)
    k_out = pltpu.make_async_copy(nk_s, out_k, out_sem.at[0])
    v_out = pltpu.make_async_copy(nv_s, out_v, out_sem.at[1])
    k_out.start()
    v_out.start()

    wait(sbuf, s_sem.at[1])
    wait(obuf, o_sem.at[1])
    peaks = sbuf[:, :, :HEAD_DIM]
    highest = jnp.max(peaks, axis=0)
    shares = jnp.exp(peaks - highest[None])
    sums = jnp.sum(shares * sbuf[:, :, HEAD_DIM:], axis=0)
    here = lane == zz * ROWS + iota(chunk, 0)

    def column(row):
        return jnp.sum(jnp.where(here, row, 0.0), axis=1, keepdims=True)

    top = column(highest)
    merged = None
    for s in range(NX * NZ):
        part = column(shares[s]) * obuf[s].astype(F32)
        merged = part if s == 0 else merged + part
    best = jnp.maximum(top, d_peak)
    c_share = jnp.exp(top - best)
    d_share = jnp.exp(d_peak - best)
    attention = (merged * c_share + d_out * d_share) / (column(sums) * c_share + d_sum * d_share)
    att_s[...] = attention
    att4 = jnp.concatenate([att_s[h * OWN : (h + 1) * OWN, :] for h in range(HEADS)], axis=1).astype(BF16)

    c_wo.wait()
    for n in range(NT):
        pr_s[n * OWN : (n + 1) * OWN, :] = dot(att4, wo_s[:, n * WIDTH : (n + 1) * WIDTH])
    pr_send[...] = pr_s[...].astype(BF16)
    for i, peer in enumerate(y_peers):
        remote(pr_send, pr_recv.at[i], p_sem.at[0], p_sem.at[1], peer)
    c_pg.wait()
    wait(pr_recv, p_sem.at[1])
    whole = pr_s[...] + pr_recv[0].astype(F32) + pr_recv[1].astype(F32) + pr_recv[2].astype(F32)
    pr_s[...] = whole
    quarters = [pr_s[n * OWN : (n + 1) * OWN, :] for n in range(NT)]
    squares = sum(part * part for part in quarters)
    power = jnp.sum(squares, axis=1, keepdims=True)
    own = quarters[0]
    for n in range(1, NT):
        own = jnp.where(tp == n, quarters[n], own)
    normed = own * lax.rsqrt(power / (NT * WIDTH) + EPS) * pg_s[...]
    residual = hid_s[:, pl.ds(pl.multiple_of(tp * WIDTH, WIDTH), WIDTH)].astype(F32)
    oh_s[...] = (residual + normed).astype(BF16)
    h_out = pltpu.make_async_copy(oh_s, out_h, out_sem.at[2])
    h_out.start()

    wait(sq_recv, sq_sem.at[0])
    wait(kfull.at[:, mine, :], swap_sem.at[0])
    wait(vfull.at[:, mine, :], swap_sem.at[2])
    wait(qbuf.at[pl.ds(0, NX * NZ - 1)], q_send)
    wait(kbuf.at[0, 0, pl.ds(0, NZ - 1)], z_sem.at[0])
    wait(vbuf.at[0, 0, pl.ds(0, NZ - 1)], z_sem.at[2])
    wait(kbuf.at[0, pl.ds(0, NX - 1)], x_sem.at[0])
    wait(vbuf.at[0, pl.ds(0, NX - 1)], x_sem.at[1])
    for i in range(NX):
        wait(kbuf.at[0, 0], c_sem.at[4 * i])
        wait(vbuf.at[0, 0], c_sem.at[4 * i + 2])
    wait(sbuf.at[pl.ds(0, NX * NZ - 1)], s_sem.at[0])
    wait(obuf.at[pl.ds(0, NX * NZ - 1)], o_sem.at[0])
    wait(pr_recv, p_sem.at[0])
    k_out.wait()
    v_out.wait()
    h_out.wait()


def body(hid, wq, wk, wv, wo, qg, kg, pg, kc, vc, lens, parents, leaf):
    half = np.arange(HEAD_DIM // 2, dtype=np.float32)
    freqs = np.power(np.float32(THETA), np.float32(-2.0) * half / np.float32(HEAD_DIM)).astype(np.float32)
    freq = jnp.asarray(np.concatenate([freqs, freqs])[None])
    vmem, sems = pltpu.VMEM, pltpu.SemaphoreType.DMA
    full = NC * BLOCK
    scratch = [
        vmem(hid.shape, BF16), vmem(wq.shape, BF16), vmem(wk.shape, BF16), vmem(wv.shape, BF16), vmem(wo.shape, BF16),
        vmem((1, WIDTH), F32), vmem((1, WIDTH), F32), vmem((1, WIDTH), F32),
        vmem(parents.shape, jnp.int32), vmem((1, HEAD_DIM), F32),
        pltpu.SMEM(lens.shape, jnp.int32), pltpu.SMEM(leaf.shape, jnp.int32),
        vmem((REQ, full, WIDTH), BF16), vmem((REQ, full, WIDTH), BF16), vmem((REQ, DRAFT, DRAFT), BF16),
        vmem((8, HEAD_DIM), F32), vmem((NT - 1, 8, HEAD_DIM), F32),
        vmem((ROWS, HEAD_DIM), BF16), vmem((ROWS, HEAD_DIM), BF16), vmem((ROWS, HEAD_DIM), BF16),
        vmem((NX * NZ, ROWS, HEAD_DIM), BF16),
        vmem((NC, NX, NZ, ROWS, HEAD_DIM), BF16), vmem((NC, NX, NZ, ROWS, HEAD_DIM), BF16),
        vmem((NX, NZ, ROWS, HEAD_DIM), BF16), vmem((NX, 1, 2 * HEAD_DIM), F32),
        vmem((NX * NZ, ROWS, HEAD_DIM), BF16), vmem((NX * NZ, 1, 2 * HEAD_DIM), F32),
        vmem((ROWS, HEAD_DIM), F32), vmem((ROWS, WIDTH), F32),
        vmem((ROWS, WIDTH), BF16), vmem((NT - 1, ROWS, WIDTH), BF16),
        vmem((REQ, BLOCK, WIDTH), BF16), vmem((REQ, BLOCK, WIDTH), BF16), vmem((OWN, WIDTH), BF16),
        sems((14,)), sems((4,)), sems((2,)), sems((NX,)), sems, sems((4,)), sems((8,)), sems((16,)),
        sems((2,)), sems((2,)), sems((2,)), sems((3,)),
    ]
    anywhere = pl.BlockSpec(memory_space=pltpu.HBM)
    return pl.pallas_call(
        kernel,
        out_shape=(
            jax.ShapeDtypeStruct((OWN, WIDTH), BF16),
            jax.ShapeDtypeStruct(kc.shape, BF16),
            jax.ShapeDtypeStruct(vc.shape, BF16),
        ),
        in_specs=[anywhere] * 14,
        out_specs=(anywhere,) * 3,
        scratch_shapes=scratch,
        compiler_params=pltpu.CompilerParams(
            collective_id=0, has_side_effects=True, vmem_limit_bytes=63 * 1024 * 1024
        ),
        cost_estimate=pl.CostEstimate(flops=300000000, bytes_accessed=11000000, transcendentals=200000),
        name="tree_attention",
    )(
        hid, wq, wk, wv, wo, qg.reshape(1, WIDTH), kg.reshape(1, WIDTH), pg.reshape(1, WIDTH),
        kc, vc, lens, parents, leaf, freq,
    )


def solution(mesh):
    return jax.shard_map(
        body,
        mesh=mesh,
        in_specs=(
            P("seq", None),
            P(None, "tp"),
            P(None, "tp"),
            P(None, "tp"),
            P("tp", None),
            P("tp"),
            P("tp"),
            P("tp"),
            P(None, "seq", "tp"),
            P(None, "seq", "tp"),
            P(),
            P(),
            P(),
        ),
        out_specs=(P("seq", "tp"), P(None, "seq", "tp"), P(None, "seq", "tp")),
        check_vma=False,
    )
```

```python
import math

import jax
import jax.numpy as jnp
import numpy as np
from jax import lax
from jax.experimental import pallas as pl
from jax.experimental.pallas import tpu as pltpu
from jax.sharding import PartitionSpec as P

HEAD_DIM = 128
EPS = 1e-06
THETA = 500000.0
NEG = -1e30
NX, NZ, NC, NT = 4, 8, 2, 4
HEADS = 4
OWN = 4
ROWS = HEADS * OWN
DRAFT = 64
REQ = 4
WIDTH = HEADS * HEAD_DIM
BLOCK = 128
MESH = pl.DeviceIdType.MESH
F32 = jnp.float32
BF16 = jnp.bfloat16
VMEM1 = 48 * 1024 * 1024
VMEM2 = 16 * 1024 * 1024
PLANES = (0, 1, 3, 2)
FAR_Z = (4, 3, 5, 2, 6, 1, 7, 0)


def far_first():
    hops = lambda a, b: min(a, NX - a) + min(b, NZ - b)
    pairs = [(a, b) for a in range(NX) for b in range(NZ) if (a, b) != (0, 0)]
    return sorted(pairs, key=lambda pair: -hops(*pair))


def iota(shape, dim):
    return lax.broadcasted_iota(jnp.int32, shape, dim)


def nt_dot(a, b):
    return lax.dot_general(a, b, (((1,), (1,)), ((), ())), preferred_element_type=F32)


def dot(a, b):
    return jnp.dot(a, b, preferred_element_type=F32)


def kernel(
    hid, wq, wk, wv, wo, qg, kg, pg, kc, vc, lens, par, leaf, freq,
    out_h, out_k, out_v,
    hid_s, wq_s, wk_s, wv_s, wo_s, qg_s, kg_s, pg_s, par_s, freq_s, lens_s, leaf_s,
    kfull, vfull, anc_s, sq_send, sq_recv, q_own, k_own, v_own, qbuf, kbuf, vbuf,
    o_st, s_st, obuf, sbuf, att_s, pr_s, pr_send, pr_recv,
    lsem, swap_sem, sq_sem, q_sem, q_send, z_sem, x_sem, c_sem, o_sem, s_sem, p_sem, plane_sem,
):
    seq = lax.axis_index("seq")
    tp = lax.axis_index("tp")
    core = lax.rem(seq, NC)
    zz = lax.rem(seq // NC, NZ)
    xx = seq // (NC * NZ)

    def at(dx, dz):
        return ((lax.rem(xx + dx, NX) * NZ + lax.rem(zz + dz, NZ)) * NC + core, tp)

    partner = (seq + 1 - 2 * core, tp)
    y_peers = [(seq, lax.rem(tp + d, NT)) for d in range(1, NT)]
    plane_peers = [at(a, b) for a, b in far_first()]
    x_peers = [at(a, 0) for a in range(1, NX)]
    near_peers = [at(0, b) for b in range(1, NZ)] + x_peers + y_peers + [partner]

    barrier = pltpu.get_barrier_semaphore()
    for peer in near_peers:
        pl.semaphore_signal(barrier, inc=1, device_id=peer, device_id_type=MESH)

    pairs = [
        (par, par_s), (hid, hid_s), (wq, wq_s), (lens, lens_s), (freq, freq_s), (qg, qg_s), (kg, kg_s),
        (wk, wk_s), (wv, wv_s), (pg, pg_s), (leaf, leaf_s),
        (kc, kfull.at[:, pl.ds(core * BLOCK, BLOCK), :]),
        (vc, vfull.at[:, pl.ds(core * BLOCK, BLOCK), :]),
        (wo, wo_s),
    ]
    local = [pltpu.make_async_copy(a, b, lsem.at[i]) for i, (a, b) in enumerate(pairs)]
    for copy in local:
        copy.start()
    (c_par, c_hid, c_wq, c_lens, c_freq, c_qg, c_kg, c_wk, c_wv, c_pg, c_leaf, c_kc, c_vc, c_wo) = local

    def remote(src, dst, send, recv, peer):
        copy = pltpu.make_async_remote_copy(
            src_ref=src, dst_ref=dst, send_sem=send, recv_sem=recv, device_id=peer, device_id_type=MESH
        )
        copy.start()

    def wait(ref, sem):
        pltpu.make_async_copy(ref, ref, sem).wait()

    c_par.wait()
    square = (DRAFT, DRAFT)
    eye = (iota(square, 0) == iota(square, 1)).astype(F32)
    chains = []
    for r in range(REQ):
        up = (par_s[pl.ds(r, 1), :] == iota(square, 0)).astype(F32)
        chains.append((eye + up).astype(BF16))
    for _ in range(6):
        chains = [jnp.minimum(dot(a, a), 1.0).astype(BF16) for a in chains]
    for r in range(REQ):
        anc_s[r] = chains[r]

    chunk = (ROWS, HEAD_DIM)
    row_head = (iota(chunk, 0) >> 2) & 3
    lane = iota(chunk, 1)
    row_token = (zz * NC + core) * OWN + (iota((ROWS, DRAFT), 0) & 3)
    one_hot = (iota((ROWS, DRAFT), 1) == row_token).astype(F32).astype(BF16)
    anc_rows = nt_dot(one_hot, anc_s[xx])
    depth = jnp.sum(anc_rows, axis=1, keepdims=True) - 1.0
    c_lens.wait()
    position = lens_s[xx].astype(F32) + depth
    c_freq.wait()
    angle = position * freq_s[...]
    cosine = jnp.cos(angle)
    sine = jnp.sin(angle)
    sine = jnp.where(lane < HEAD_DIM // 2, -sine, sine)

    c_hid.wait()
    h4 = hid_s[...].astype(F32)
    h8 = jnp.concatenate([h4, h4], axis=0)
    h16 = jnp.concatenate([h8, h8], axis=0).astype(BF16)

    def diagonal(wide):
        picked = wide[:, :HEAD_DIM]
        for h in range(1, HEADS):
            picked = jnp.where(row_head == h, wide[:, h * HEAD_DIM : (h + 1) * HEAD_DIM], picked)
        return picked

    def spread(gain):
        return diagonal(jnp.broadcast_to(gain, (ROWS, WIDTH)))

    lane8 = iota((8, HEAD_DIM), 1)

    def turned(wide, gain):
        x = diagonal(wide) * spread(gain)
        return x * cosine + pltpu.roll(x, HEAD_DIM // 2, 1) * sine

    def square_sum(wide):
        return jnp.broadcast_to(jnp.sum(wide * wide, axis=1, keepdims=True)[:8], (8, HEAD_DIM))

    def scaled(x, i):
        wait(sq_recv.at[i], sq_sem.at[2 * i + 1])
        total = sq_send[i] + sq_recv[i, 0] + sq_recv[i, 1] + sq_recv[i, 2]
        scale = lax.rsqrt(total / (NT * WIDTH) + EPS)
        return (x * jnp.concatenate([scale, scale], axis=0)).astype(BF16)

    c_wq.wait()
    q_wide = dot(h16, wq_s[...])
    sq_send[0] = square_sum(q_wide)

    pl.semaphore_wait(barrier, len(near_peers))
    for i, peer in enumerate(y_peers):
        remote(sq_send.at[0], sq_recv.at[0, i], sq_sem.at[0], sq_sem.at[1], peer)
    for peer in x_peers:
        pl.semaphore_signal(plane_sem, inc=1, device_id=peer, device_id_type=MESH)

    for copy in (c_qg, c_kg):
        copy.wait()
    q_turn = turned(q_wide, qg_s[...])
    c_wk.wait()
    k_wide = dot(h16, wk_s[...])
    sq_send[1] = square_sum(k_wide)
    for i, peer in enumerate(y_peers):
        remote(sq_send.at[1], sq_recv.at[1, i], sq_sem.at[2], sq_sem.at[3], peer)
    mine = pl.ds(core * BLOCK, BLOCK)
    remote(kc, kfull.at[:, mine, :], swap_sem.at[0], swap_sem.at[1], partner)
    remote(vc, vfull.at[:, mine, :], swap_sem.at[2], swap_sem.at[3], partner)
    k_turn = turned(k_wide, kg_s[...])
    c_wv.wait()
    v_own[...] = diagonal(dot(h16, wv_s[...])).astype(BF16)

    q_own[...] = scaled(q_turn, 0)
    pl.semaphore_wait(plane_sem, len(x_peers))

    for peer in plane_peers:
        remote(q_own, qbuf.at[xx * NZ + zz], q_send, q_sem.at[xx], peer)
    pltpu.make_async_copy(q_own, qbuf.at[xx * NZ + zz], q_sem.at[xx]).start()
    k_own[...] = scaled(k_turn, 1)
    for dz in FAR_Z[:-1]:
        remote(k_own, kbuf.at[core, xx, zz], z_sem.at[0], z_sem.at[1], at(0, dz))
        remote(v_own, vbuf.at[core, xx, zz], z_sem.at[2], z_sem.at[3], at(0, dz))
    pltpu.make_async_copy(k_own, kbuf.at[core, xx, zz], z_sem.at[1]).start()
    pltpu.make_async_copy(v_own, vbuf.at[core, xx, zz], z_sem.at[3]).start()

    factor = 1.0 / math.sqrt(HEAD_DIM)
    tall = (NZ * ROWS, NC * BLOCK)
    tall_head = (iota(tall, 0) >> 2) & 3
    place = (seq - core) * BLOCK + iota(tall, 1)
    turn = iota((NZ * ROWS, HEAD_DIM), 0) == iota((NZ * ROWS, HEAD_DIM), 1)
    c_kc.wait()
    c_vc.wait()
    wait(kfull.at[:, mine, :], swap_sem.at[1])
    wait(vfull.at[:, mine, :], swap_sem.at[3])
    for step, dx in enumerate(PLANES):
        r = lax.rem(xx + dx, NX)
        group = pl.ds(r * NZ, NZ)
        wait(qbuf.at[group], q_sem.at[r])
        queries = qbuf[group].reshape(NZ * ROWS, HEAD_DIM)
        scores = None
        for h in range(HEADS):
            part = nt_dot(queries, kfull[r, :, h * HEAD_DIM : (h + 1) * HEAD_DIM])
            scores = part if h == 0 else jnp.where(tall_head == h, part, scores)
        visible = place < lens_s[r]
        scores = jnp.where(visible, scores * factor, NEG)
        peak = jnp.max(scores, axis=1, keepdims=True)
        weights = jnp.where(visible, jnp.exp(scores - peak), 0.0)
        weight_sum = jnp.sum(weights, axis=1, keepdims=True)
        mixed = None
        for h in range(HEADS):
            masked = jnp.where(tall_head == h, weights, 0.0).astype(BF16)
            part = dot(masked, vfull[r, :, h * HEAD_DIM : (h + 1) * HEAD_DIM])
            mixed = part if h == 0 else mixed + part
        o_st[step] = mixed.astype(BF16).reshape(NZ, ROWS, HEAD_DIM)
        s_st[step, :, :HEAD_DIM] = jnp.sum(jnp.where(turn, peak, 0.0), axis=0, keepdims=True)
        s_st[step, :, HEAD_DIM:] = jnp.sum(jnp.where(turn, weight_sum, 0.0), axis=0, keepdims=True)
        slot = xx * NZ + zz
        for dz in FAR_Z:
            to = lax.rem(zz + dz, NZ)
            if (dx, dz) == (0, 0):
                pltpu.make_async_copy(o_st.at[step, to], obuf.at[slot], o_sem.at[1]).start()
                pltpu.make_async_copy(s_st.at[step], sbuf.at[slot], s_sem.at[1]).start()
            else:
                remote(s_st.at[step], sbuf.at[slot], s_sem.at[0], s_sem.at[1], at(dx, dz))
                remote(o_st.at[step, to], obuf.at[slot], o_sem.at[0], o_sem.at[1], at(dx, dz))

    wait(kbuf.at[core, xx], z_sem.at[1])
    wait(vbuf.at[core, xx], z_sem.at[3])
    remote(kbuf.at[core, xx], kbuf.at[core, xx], c_sem.at[0], c_sem.at[1], partner)
    remote(vbuf.at[core, xx], vbuf.at[core, xx], c_sem.at[2], c_sem.at[3], partner)
    for dx in (2, 1, 3):
        remote(kbuf.at[core, xx], kbuf.at[core, xx], x_sem.at[0], x_sem.at[1 + dx], at(dx, 0))
        remote(vbuf.at[core, xx], vbuf.at[core, xx], x_sem.at[1], x_sem.at[4 + dx], at(dx, 0))

    wait(kbuf.at[core, xx], c_sem.at[1])
    wait(vbuf.at[core, xx], c_sem.at[3])
    both = NC * NZ * ROWS
    col = iota((DRAFT, both), 1)
    col_token = ((col >> 4) & 7) * (NC * OWN) + (col >> 7) * OWN + (col & 3)
    expand = (iota((DRAFT, both), 0) == col_token).astype(F32).astype(BF16)
    allowed = dot(anc_rows.astype(BF16), expand) > 0.5
    wide_shape = (ROWS, both)
    allowed = allowed & (((iota(wide_shape, 1) >> 2) & 3) == ((iota(wide_shape, 0) >> 2) & 3))

    def request_rows(buf, r):
        return jnp.concatenate([buf[c, r].reshape(NZ * ROWS, HEAD_DIM) for c in range(NC)], axis=0)

    d_scores = jnp.where(allowed, nt_dot(q_own[...], request_rows(kbuf, xx)) * factor, NEG)
    d_peak = jnp.max(d_scores, axis=1, keepdims=True)
    d_weights = jnp.where(allowed, jnp.exp(d_scores - d_peak), 0.0)
    d_sum = jnp.sum(d_weights, axis=1, keepdims=True)
    d_out = dot(d_weights.astype(BF16), request_rows(vbuf, xx))

    for i, dx in enumerate((1, 3, 2)):
        r = lax.rem(xx + dx, NX)
        wait(kbuf.at[core, r], x_sem.at[1 + (NX - dx)])
        wait(vbuf.at[core, r], x_sem.at[4 + (NX - dx)])
        remote(kbuf.at[core, r], kbuf.at[core, r], c_sem.at[4 + 4 * i], c_sem.at[5 + 4 * i], partner)
        remote(vbuf.at[core, r], vbuf.at[core, r], c_sem.at[6 + 4 * i], c_sem.at[7 + 4 * i], partner)

    c_leaf.wait()
    p_place = (seq * BLOCK + iota((BLOCK, DRAFT), 0)).astype(F32)
    col_head = (iota((BLOCK, both), 1) >> 2) & 3

    def compact(i, dx):
        r = lax.rem(xx + dx, NX)
        if dx:
            wait(kbuf.at[core, r], c_sem.at[1 + 4 * i])
            wait(vbuf.at[core, r], c_sem.at[3 + 4 * i])
        anc = anc_s[r]
        target = jnp.sum(anc.astype(F32), axis=0, keepdims=True) - 1.0 + lens_s[r].astype(F32)
        leaf_hot = (iota((ROWS, DRAFT), 1) == leaf_s[r]).astype(F32).astype(BF16)
        on_path = nt_dot(leaf_hot, anc)[:1]
        placing = jnp.where((p_place == target) & (on_path > 0.5), 1.0, 0.0)
        written = jnp.sum(placing, axis=1, keepdims=True) > 0.5
        placing = dot(placing.astype(BF16), expand)
        k_rows = request_rows(kbuf, r)
        v_rows = request_rows(vbuf, r)
        for h in range(HEADS):
            columns = slice(h * HEAD_DIM, (h + 1) * HEAD_DIM)
            pick = jnp.where(col_head == h, placing, 0.0).astype(BF16)
            old_k = kfull[r, mine, columns].astype(F32)
            old_v = vfull[r, mine, columns].astype(F32)
            out_k[r, :, columns] = jnp.where(written, dot(pick, k_rows), old_k).astype(BF16)
            out_v[r, :, columns] = jnp.where(written, dot(pick, v_rows), old_v).astype(BF16)

    compact(0, 0)

    wait(sbuf, s_sem.at[1])
    wait(obuf, o_sem.at[1])
    peaks = sbuf[:, :, :HEAD_DIM]
    highest = jnp.max(peaks, axis=0)
    shares = jnp.exp(peaks - highest[None])
    sums = jnp.sum(shares * sbuf[:, :, HEAD_DIM:], axis=0)
    here = lane == zz * ROWS + iota(chunk, 0)

    def column(row):
        return jnp.sum(jnp.where(here, row, 0.0), axis=1, keepdims=True)

    top = column(highest)
    merged = None
    for s in range(NX * NZ):
        part = column(shares[s]) * obuf[s].astype(F32)
        merged = part if s == 0 else merged + part
    best = jnp.maximum(top, d_peak)
    c_share = jnp.exp(top - best)
    d_share = jnp.exp(d_peak - best)
    attention = (merged * c_share + d_out * d_share) / (column(sums) * c_share + d_sum * d_share)
    att_s[...] = attention
    att4 = jnp.concatenate([att_s[h * OWN : (h + 1) * OWN, :] for h in range(HEADS)], axis=1).astype(BF16)

    c_wo.wait()
    for n in range(NT):
        pr_s[n * OWN : (n + 1) * OWN, :] = dot(att4, wo_s[:, n * WIDTH : (n + 1) * WIDTH])
    pr_send[...] = pr_s[...].astype(BF16)
    for i, peer in enumerate(y_peers):
        remote(pr_send, pr_recv.at[i], p_sem.at[0], p_sem.at[1], peer)
    for i, dx in enumerate((1, 3, 2)):
        compact(i + 1, dx)
    c_pg.wait()
    wait(pr_recv, p_sem.at[1])
    whole = pr_s[...] + pr_recv[0].astype(F32) + pr_recv[1].astype(F32) + pr_recv[2].astype(F32)
    pr_s[...] = whole
    quarters = [pr_s[n * OWN : (n + 1) * OWN, :] for n in range(NT)]
    squares = sum(part * part for part in quarters)
    power = jnp.sum(squares, axis=1, keepdims=True)
    own = quarters[0]
    for n in range(1, NT):
        own = jnp.where(tp == n, quarters[n], own)
    normed = own * lax.rsqrt(power / (NT * WIDTH) + EPS) * pg_s[...]
    residual = hid_s[:, pl.ds(pl.multiple_of(tp * WIDTH, WIDTH), WIDTH)].astype(F32)
    out_h[...] = (residual + normed).astype(BF16)

    wait(sq_recv.at[0], sq_sem.at[0])
    wait(sq_recv.at[1], sq_sem.at[2])
    wait(kfull.at[:, mine, :], swap_sem.at[0])
    wait(vfull.at[:, mine, :], swap_sem.at[2])
    wait(qbuf.at[pl.ds(0, NX * NZ - 1)], q_send)
    wait(kbuf.at[0, 0, pl.ds(0, NZ - 1)], z_sem.at[0])
    wait(vbuf.at[0, 0, pl.ds(0, NZ - 1)], z_sem.at[2])
    wait(kbuf.at[0, pl.ds(0, NX - 1)], x_sem.at[0])
    wait(vbuf.at[0, pl.ds(0, NX - 1)], x_sem.at[1])
    for i in range(NX):
        wait(kbuf.at[0, 0], c_sem.at[4 * i])
        wait(vbuf.at[0, 0], c_sem.at[4 * i + 2])
    wait(sbuf.at[pl.ds(0, NX * NZ - 1)], s_sem.at[0])
    wait(obuf.at[pl.ds(0, NX * NZ - 1)], o_sem.at[0])
    wait(pr_recv, p_sem.at[0])


def hand_out(a, b, c, out_a, out_b, out_c, sem):
    copies = [
        pltpu.make_async_copy(src, dst, sem.at[i])
        for i, (src, dst) in enumerate(((b, out_b), (c, out_c), (a, out_a)))
    ]
    for copy in copies:
        copy.start()
    for copy in copies:
        copy.wait()


def body(hid, wq, wk, wv, wo, qg, kg, pg, kc, vc, lens, parents, leaf):
    half = np.arange(HEAD_DIM // 2, dtype=np.float32)
    freqs = np.power(np.float32(THETA), np.float32(-2.0) * half / np.float32(HEAD_DIM)).astype(np.float32)
    freq = jnp.asarray(np.concatenate([freqs, freqs])[None])
    vmem, sems = pltpu.VMEM, pltpu.SemaphoreType.DMA
    full = NC * BLOCK
    scratch = [
        vmem(hid.shape, BF16), vmem(wq.shape, BF16), vmem(wk.shape, BF16), vmem(wv.shape, BF16), vmem(wo.shape, BF16),
        vmem((1, WIDTH), F32), vmem((1, WIDTH), F32), vmem((1, WIDTH), F32),
        vmem(parents.shape, jnp.int32), vmem((1, HEAD_DIM), F32),
        pltpu.SMEM(lens.shape, jnp.int32), pltpu.SMEM(leaf.shape, jnp.int32),
        vmem((REQ, full, WIDTH), BF16), vmem((REQ, full, WIDTH), BF16), vmem((REQ, DRAFT, DRAFT), BF16),
        vmem((2, 8, HEAD_DIM), F32), vmem((2, NT - 1, 8, HEAD_DIM), F32),
        vmem((ROWS, HEAD_DIM), BF16), vmem((ROWS, HEAD_DIM), BF16), vmem((ROWS, HEAD_DIM), BF16),
        vmem((NX * NZ, ROWS, HEAD_DIM), BF16),
        vmem((NC, NX, NZ, ROWS, HEAD_DIM), BF16), vmem((NC, NX, NZ, ROWS, HEAD_DIM), BF16),
        vmem((NX, NZ, ROWS, HEAD_DIM), BF16), vmem((NX, 1, 2 * HEAD_DIM), F32),
        vmem((NX * NZ, ROWS, HEAD_DIM), BF16), vmem((NX * NZ, 1, 2 * HEAD_DIM), F32),
        vmem((ROWS, HEAD_DIM), F32), vmem((ROWS, WIDTH), F32),
        vmem((ROWS, WIDTH), BF16), vmem((NT - 1, ROWS, WIDTH), BF16),
        sems((14,)), sems((4,)), sems((4,)), sems((NX,)), sems, sems((4,)), sems((8,)), sems((16,)),
        sems((2,)), sems((2,)), sems((2,)), pltpu.SemaphoreType.REGULAR,
    ]
    anywhere = pl.BlockSpec(memory_space=pltpu.HBM)
    results = pl.pallas_call(
        kernel,
        out_shape=(vmem((OWN, WIDTH), BF16), vmem(kc.shape, BF16), vmem(vc.shape, BF16)),
        in_specs=[anywhere] * 14,
        out_specs=(pl.BlockSpec(memory_space=pltpu.VMEM),) * 3,
        scratch_shapes=scratch,
        compiler_params=pltpu.CompilerParams(
            collective_id=0, has_side_effects=True, vmem_limit_bytes=VMEM1
        ),
        cost_estimate=pl.CostEstimate(flops=300000000, bytes_accessed=11000000, transcendentals=200000),
        name="tree_attention",
    )(*(pltpu.with_memory_space_constraint(part, pltpu.HBM) for part in (
        hid, wq, wk, wv, wo, qg.reshape(1, WIDTH), kg.reshape(1, WIDTH), pg.reshape(1, WIDTH),
        kc, vc, lens, parents, leaf, freq,
    )))
    return pl.pallas_call(
        hand_out,
        out_shape=tuple(jax.ShapeDtypeStruct(part.shape, part.dtype) for part in results),
        in_specs=[pl.BlockSpec(memory_space=pltpu.VMEM)] * 3,
        out_specs=(anywhere,) * 3,
        scratch_shapes=[sems((3,))],
        compiler_params=pltpu.CompilerParams(vmem_limit_bytes=VMEM2),
        cost_estimate=pl.CostEstimate(flops=0, bytes_accessed=2200000, transcendentals=0),
        name="hand_out",
    )(*results)


def solution(mesh):
    return jax.shard_map(
        body,
        mesh=mesh,
        in_specs=(
            P("seq", None),
            P(None, "tp"),
            P(None, "tp"),
            P(None, "tp"),
            P("tp", None),
            P("tp"),
            P("tp"),
            P("tp"),
            P(None, "seq", "tp"),
            P(None, "seq", "tp"),
            P(),
            P(),
            P(),
        ),
        out_specs=(P("seq", "tp"), P(None, "seq", "tp"), P(None, "seq", "tp")),
        check_vma=False,
    )
```

```python
import math

import jax
import jax.numpy as jnp
import numpy as np
from jax import lax
from jax.experimental import pallas as pl
from jax.experimental.pallas import tpu as pltpu
from jax.sharding import PartitionSpec as P

HEAD_DIM = 128
EPS = 1e-06
THETA = 500000.0
NEG = -1e30
NX, NZ, NC, NT = 4, 8, 2, 4
HEADS = 4
OWN = 4
ROWS = HEADS * OWN
DRAFT = 64
REQ = 4
WIDTH = HEADS * HEAD_DIM
BLOCK = 128
MESH = pl.DeviceIdType.MESH
F32 = jnp.float32
BF16 = jnp.bfloat16
VMEM1 = 48 * 1024 * 1024
VMEM2 = 16 * 1024 * 1024
PLANES = (2, 1, 3, 0)
FAR_Z = (4, 3, 5, 2, 6, 1, 7, 0)


def far_first():
    hops = lambda a, b: min(a, NX - a) + min(b, NZ - b)
    pairs = [(a, b) for a in range(NX) for b in range(NZ) if (a, b) != (0, 0)]
    return sorted(pairs, key=lambda pair: -hops(*pair))


def iota(shape, dim):
    return lax.broadcasted_iota(jnp.int32, shape, dim)


def nt_dot(a, b):
    return lax.dot_general(a, b, (((1,), (1,)), ((), ())), preferred_element_type=F32)


def dot(a, b):
    return jnp.dot(a, b, preferred_element_type=F32)


def kernel(
    hid, wq, wk, wv, wo, qg, kg, pg, kc, vc, lens, par, leaf, freq,
    out_h, out_k, out_v,
    hid_s, wq_s, wk_s, wv_s, wo_s, qg_s, kg_s, pg_s, par_s, freq_s, lens_s, leaf_s,
    kfull, vfull, anc_s, sq_send, sq_recv, q_own, k_own, v_own, qbuf, kbuf, vbuf,
    o_st, s_st, obuf, sbuf, att_s, pr_s, pr_send, pr_recv,
    lsem, swap_sem, sq_sem, q_sem, q_send, z_sem, x_sem, c_sem, o_sem, s_sem, p_sem, plane_sem,
):
    seq = lax.axis_index("seq")
    tp = lax.axis_index("tp")
    core = lax.rem(seq, NC)
    zz = lax.rem(seq // NC, NZ)
    xx = seq // (NC * NZ)

    def at(dx, dz):
        return ((lax.rem(xx + dx, NX) * NZ + lax.rem(zz + dz, NZ)) * NC + core, tp)

    partner = (seq + 1 - 2 * core, tp)
    y_peers = [(seq, lax.rem(tp + d, NT)) for d in range(1, NT)]
    plane_peers = [at(a, b) for a, b in far_first()]
    x_peers = [at(a, 0) for a in range(1, NX)]
    near_peers = [at(0, b) for b in range(1, NZ)] + x_peers + y_peers + [partner]

    barrier = pltpu.get_barrier_semaphore()
    for peer in near_peers:
        pl.semaphore_signal(barrier, inc=1, device_id=peer, device_id_type=MESH)

    pairs = [
        (par, par_s), (hid, hid_s), (wq, wq_s), (lens, lens_s), (freq, freq_s), (qg, qg_s), (kg, kg_s),
        (wk, wk_s), (wv, wv_s), (pg, pg_s), (leaf, leaf_s),
        (kc, kfull.at[:, pl.ds(core * BLOCK, BLOCK), :]),
        (vc, vfull.at[:, pl.ds(core * BLOCK, BLOCK), :]),
        (wo, wo_s),
    ]
    local = [pltpu.make_async_copy(a, b, lsem.at[i]) for i, (a, b) in enumerate(pairs)]
    for copy in local:
        copy.start()
    (c_par, c_hid, c_wq, c_lens, c_freq, c_qg, c_kg, c_wk, c_wv, c_pg, c_leaf, c_kc, c_vc, c_wo) = local

    def remote(src, dst, send, recv, peer):
        copy = pltpu.make_async_remote_copy(
            src_ref=src, dst_ref=dst, send_sem=send, recv_sem=recv, device_id=peer, device_id_type=MESH
        )
        copy.start()

    def wait(ref, sem):
        pltpu.make_async_copy(ref, ref, sem).wait()

    c_par.wait()
    square = (DRAFT, DRAFT)
    eye = (iota(square, 0) == iota(square, 1)).astype(F32)
    chains = []
    for r in range(REQ):
        up = (par_s[pl.ds(r, 1), :] == iota(square, 0)).astype(F32)
        chains.append((eye + up).astype(BF16))
    for _ in range(6):
        chains = [jnp.minimum(dot(a, a), 1.0).astype(BF16) for a in chains]
    for r in range(REQ):
        anc_s[r] = chains[r]

    chunk = (ROWS, HEAD_DIM)
    row_head = (iota(chunk, 0) >> 2) & 3
    lane = iota(chunk, 1)
    row_token = (zz * NC + core) * OWN + (iota((ROWS, DRAFT), 0) & 3)
    one_hot = (iota((ROWS, DRAFT), 1) == row_token).astype(F32).astype(BF16)
    anc_rows = nt_dot(one_hot, anc_s[xx])
    depth = jnp.sum(anc_rows, axis=1, keepdims=True) - 1.0
    c_lens.wait()
    position = lens_s[xx].astype(F32) + depth
    c_freq.wait()
    angle = position * freq_s[...]
    cosine = jnp.cos(angle)
    sine = jnp.sin(angle)
    sine = jnp.where(lane < HEAD_DIM // 2, -sine, sine)

    c_hid.wait()
    h4 = hid_s[...].astype(F32)
    h8 = jnp.concatenate([h4, h4], axis=0)
    h16 = jnp.concatenate([h8, h8], axis=0).astype(BF16)

    def diagonal(wide):
        picked = wide[:, :HEAD_DIM]
        for h in range(1, HEADS):
            picked = jnp.where(row_head == h, wide[:, h * HEAD_DIM : (h + 1) * HEAD_DIM], picked)
        return picked

    def spread(gain):
        return diagonal(jnp.broadcast_to(gain, (ROWS, WIDTH)))

    lane8 = iota((8, HEAD_DIM), 1)

    def turned(wide, gain):
        x = diagonal(wide) * spread(gain)
        return x * cosine + pltpu.roll(x, HEAD_DIM // 2, 1) * sine

    def square_sum(wide):
        return jnp.broadcast_to(jnp.sum(wide * wide, axis=1, keepdims=True)[:8], (8, HEAD_DIM))

    def scaled(x, i):
        wait(sq_recv.at[i], sq_sem.at[2 * i + 1])
        total = sq_send[i] + sq_recv[i, 0] + sq_recv[i, 1] + sq_recv[i, 2]
        scale = lax.rsqrt(total / (NT * WIDTH) + EPS)
        return (x * jnp.concatenate([scale, scale], axis=0)).astype(BF16)

    c_wq.wait()
    q_wide = dot(h16, wq_s[...])
    sq_send[0] = square_sum(q_wide)

    pl.semaphore_wait(barrier, len(near_peers))
    for i, peer in enumerate(y_peers):
        remote(sq_send.at[0], sq_recv.at[0, i], sq_sem.at[0], sq_sem.at[1], peer)
    for peer in x_peers:
        pl.semaphore_signal(plane_sem, inc=1, device_id=peer, device_id_type=MESH)

    for copy in (c_qg, c_kg):
        copy.wait()
    q_turn = turned(q_wide, qg_s[...])
    c_wk.wait()
    k_wide = dot(h16, wk_s[...])
    sq_send[1] = square_sum(k_wide)
    for i, peer in enumerate(y_peers):
        remote(sq_send.at[1], sq_recv.at[1, i], sq_sem.at[2], sq_sem.at[3], peer)
    mine = pl.ds(core * BLOCK, BLOCK)
    remote(kc, kfull.at[:, mine, :], swap_sem.at[0], swap_sem.at[1], partner)
    remote(vc, vfull.at[:, mine, :], swap_sem.at[2], swap_sem.at[3], partner)
    k_turn = turned(k_wide, kg_s[...])
    c_wv.wait()
    v_own[...] = diagonal(dot(h16, wv_s[...])).astype(BF16)
    for dz in FAR_Z[:-1]:
        remote(v_own, vbuf.at[core, xx, zz], z_sem.at[2], z_sem.at[3], at(0, dz))
    pltpu.make_async_copy(v_own, vbuf.at[core, xx, zz], z_sem.at[3]).start()

    q_own[...] = scaled(q_turn, 0)
    pl.semaphore_wait(plane_sem, len(x_peers))

    for peer in plane_peers:
        remote(q_own, qbuf.at[xx * NZ + zz], q_send, q_sem.at[xx], peer)
    pltpu.make_async_copy(q_own, qbuf.at[xx * NZ + zz], q_sem.at[xx]).start()
    k_own[...] = scaled(k_turn, 1)
    for dz in FAR_Z[:-1]:
        remote(k_own, kbuf.at[core, xx, zz], z_sem.at[0], z_sem.at[1], at(0, dz))
    pltpu.make_async_copy(k_own, kbuf.at[core, xx, zz], z_sem.at[1]).start()

    def onward(buf, sem, first, at_x, at_c):
        wait(buf.at[core, xx], z_sem.at[sem])
        for far in (2, 1, 3):
            remote(buf.at[core, xx], buf.at[core, xx], x_sem.at[first], x_sem.at[at_x + far], at(far, 0))
        remote(buf.at[core, xx], buf.at[core, xx], c_sem.at[at_c], c_sem.at[at_c + 1], partner)

    factor = 1.0 / math.sqrt(HEAD_DIM)
    tall = (NZ * ROWS, NC * BLOCK)
    tall_head = (iota(tall, 0) >> 2) & 3
    place = (seq - core) * BLOCK + iota(tall, 1)
    turn = iota((NZ * ROWS, HEAD_DIM), 0) == iota((NZ * ROWS, HEAD_DIM), 1)
    c_kc.wait()
    c_vc.wait()
    wait(kfull.at[:, mine, :], swap_sem.at[1])
    wait(vfull.at[:, mine, :], swap_sem.at[3])
    for step, dx in enumerate(PLANES):
        if step == 0:
            onward(vbuf, 3, 1, 4, 2)
        if step == 3:
            onward(kbuf, 1, 0, 1, 0)
        r = lax.rem(xx + dx, NX)
        group = pl.ds(r * NZ, NZ)
        wait(qbuf.at[group], q_sem.at[r])
        queries = qbuf[group].reshape(NZ * ROWS, HEAD_DIM)
        scores = None
        for h in range(HEADS):
            part = nt_dot(queries, kfull[r, :, h * HEAD_DIM : (h + 1) * HEAD_DIM])
            scores = part if h == 0 else jnp.where(tall_head == h, part, scores)
        visible = place < lens_s[r]
        scores = jnp.where(visible, scores * factor, NEG)
        peak = jnp.max(scores, axis=1, keepdims=True)
        weights = jnp.where(visible, jnp.exp(scores - peak), 0.0)
        weight_sum = jnp.sum(weights, axis=1, keepdims=True)
        mixed = None
        for h in range(HEADS):
            masked = jnp.where(tall_head == h, weights, 0.0).astype(BF16)
            part = dot(masked, vfull[r, :, h * HEAD_DIM : (h + 1) * HEAD_DIM])
            mixed = part if h == 0 else mixed + part
        o_st[step] = mixed.astype(BF16).reshape(NZ, ROWS, HEAD_DIM)
        s_st[step, :, :HEAD_DIM] = jnp.sum(jnp.where(turn, peak, 0.0), axis=0, keepdims=True)
        s_st[step, :, HEAD_DIM:] = jnp.sum(jnp.where(turn, weight_sum, 0.0), axis=0, keepdims=True)
        slot = xx * NZ + zz
        for dz in FAR_Z:
            to = lax.rem(zz + dz, NZ)
            if (dx, dz) == (0, 0):
                pltpu.make_async_copy(o_st.at[step, to], obuf.at[slot], o_sem.at[1]).start()
                pltpu.make_async_copy(s_st.at[step], sbuf.at[slot], s_sem.at[1]).start()
            else:
                remote(s_st.at[step], sbuf.at[slot], s_sem.at[0], s_sem.at[1], at(dx, dz))
                remote(o_st.at[step, to], obuf.at[slot], o_sem.at[0], o_sem.at[1], at(dx, dz))

    wait(kbuf.at[core, xx], c_sem.at[1])
    wait(vbuf.at[core, xx], c_sem.at[3])
    both = NC * NZ * ROWS
    col = iota((DRAFT, both), 1)
    col_token = ((col >> 4) & 7) * (NC * OWN) + (col >> 7) * OWN + (col & 3)
    expand = (iota((DRAFT, both), 0) == col_token).astype(F32).astype(BF16)
    allowed = dot(anc_rows.astype(BF16), expand) > 0.5
    wide_shape = (ROWS, both)
    allowed = allowed & (((iota(wide_shape, 1) >> 2) & 3) == ((iota(wide_shape, 0) >> 2) & 3))

    def request_rows(buf, r):
        return jnp.concatenate([buf[c, r].reshape(NZ * ROWS, HEAD_DIM) for c in range(NC)], axis=0)

    d_scores = jnp.where(allowed, nt_dot(q_own[...], request_rows(kbuf, xx)) * factor, NEG)
    d_peak = jnp.max(d_scores, axis=1, keepdims=True)
    d_weights = jnp.where(allowed, jnp.exp(d_scores - d_peak), 0.0)
    d_sum = jnp.sum(d_weights, axis=1, keepdims=True)
    d_out = dot(d_weights.astype(BF16), request_rows(vbuf, xx))

    for i, dx in enumerate((1, 3, 2)):
        r = lax.rem(xx + dx, NX)
        wait(kbuf.at[core, r], x_sem.at[1 + (NX - dx)])
        wait(vbuf.at[core, r], x_sem.at[4 + (NX - dx)])
        remote(kbuf.at[core, r], kbuf.at[core, r], c_sem.at[4 + 4 * i], c_sem.at[5 + 4 * i], partner)
        remote(vbuf.at[core, r], vbuf.at[core, r], c_sem.at[6 + 4 * i], c_sem.at[7 + 4 * i], partner)

    c_leaf.wait()
    p_place = (seq * BLOCK + iota((BLOCK, DRAFT), 0)).astype(F32)
    col_head = (iota((BLOCK, both), 1) >> 2) & 3

    def compact(i, dx):
        r = lax.rem(xx + dx, NX)
        if dx:
            wait(kbuf.at[core, r], c_sem.at[1 + 4 * i])
            wait(vbuf.at[core, r], c_sem.at[3 + 4 * i])
        anc = anc_s[r]
        target = jnp.sum(anc.astype(F32), axis=0, keepdims=True) - 1.0 + lens_s[r].astype(F32)
        leaf_hot = (iota((ROWS, DRAFT), 1) == leaf_s[r]).astype(F32).astype(BF16)
        on_path = nt_dot(leaf_hot, anc)[:1]
        placing = jnp.where((p_place == target) & (on_path > 0.5), 1.0, 0.0)
        written = jnp.sum(placing, axis=1, keepdims=True) > 0.5
        placing = dot(placing.astype(BF16), expand)
        k_rows = request_rows(kbuf, r)
        v_rows = request_rows(vbuf, r)
        for h in range(HEADS):
            columns = slice(h * HEAD_DIM, (h + 1) * HEAD_DIM)
            pick = jnp.where(col_head == h, placing, 0.0).astype(BF16)
            old_k = kfull[r, mine, columns].astype(F32)
            old_v = vfull[r, mine, columns].astype(F32)
            out_k[r, :, columns] = jnp.where(written, dot(pick, k_rows), old_k).astype(BF16)
            out_v[r, :, columns] = jnp.where(written, dot(pick, v_rows), old_v).astype(BF16)

    compact(0, 0)

    wait(sbuf, s_sem.at[1])
    wait(obuf, o_sem.at[1])
    peaks = sbuf[:, :, :HEAD_DIM]
    highest = jnp.max(peaks, axis=0)
    shares = jnp.exp(peaks - highest[None])
    sums = jnp.sum(shares * sbuf[:, :, HEAD_DIM:], axis=0)
    here = lane == zz * ROWS + iota(chunk, 0)

    def column(row):
        return jnp.sum(jnp.where(here, row, 0.0), axis=1, keepdims=True)

    top = column(highest)
    merged = None
    for s in range(NX * NZ):
        part = column(shares[s]) * obuf[s].astype(F32)
        merged = part if s == 0 else merged + part
    best = jnp.maximum(top, d_peak)
    c_share = jnp.exp(top - best)
    d_share = jnp.exp(d_peak - best)
    attention = (merged * c_share + d_out * d_share) / (column(sums) * c_share + d_sum * d_share)
    att_s[...] = attention
    att4 = jnp.concatenate([att_s[h * OWN : (h + 1) * OWN, :] for h in range(HEADS)], axis=1).astype(BF16)

    c_wo.wait()
    for n in range(NT):
        pr_s[n * OWN : (n + 1) * OWN, :] = dot(att4, wo_s[:, n * WIDTH : (n + 1) * WIDTH])
    pr_send[...] = pr_s[...].astype(BF16)
    for i, peer in enumerate(y_peers):
        remote(pr_send, pr_recv.at[i], p_sem.at[0], p_sem.at[1], peer)
    for i, dx in enumerate((1, 3, 2)):
        compact(i + 1, dx)
    c_pg.wait()
    wait(pr_recv, p_sem.at[1])
    whole = pr_s[...] + pr_recv[0].astype(F32) + pr_recv[1].astype(F32) + pr_recv[2].astype(F32)
    pr_s[...] = whole
    quarters = [pr_s[n * OWN : (n + 1) * OWN, :] for n in range(NT)]
    squares = sum(part * part for part in quarters)
    power = jnp.sum(squares, axis=1, keepdims=True)
    own = quarters[0]
    for n in range(1, NT):
        own = jnp.where(tp == n, quarters[n], own)
    normed = own * lax.rsqrt(power / (NT * WIDTH) + EPS) * pg_s[...]
    residual = hid_s[:, pl.ds(pl.multiple_of(tp * WIDTH, WIDTH), WIDTH)].astype(F32)
    out_h[...] = (residual + normed).astype(BF16)

    wait(sq_recv.at[0], sq_sem.at[0])
    wait(sq_recv.at[1], sq_sem.at[2])
    wait(kfull.at[:, mine, :], swap_sem.at[0])
    wait(vfull.at[:, mine, :], swap_sem.at[2])
    wait(qbuf.at[pl.ds(0, NX * NZ - 1)], q_send)
    wait(kbuf.at[0, 0, pl.ds(0, NZ - 1)], z_sem.at[0])
    wait(vbuf.at[0, 0, pl.ds(0, NZ - 1)], z_sem.at[2])
    wait(kbuf.at[0, pl.ds(0, NX - 1)], x_sem.at[0])
    wait(vbuf.at[0, pl.ds(0, NX - 1)], x_sem.at[1])
    for i in range(NX):
        wait(kbuf.at[0, 0], c_sem.at[4 * i])
        wait(vbuf.at[0, 0], c_sem.at[4 * i + 2])
    wait(sbuf.at[pl.ds(0, NX * NZ - 1)], s_sem.at[0])
    wait(obuf.at[pl.ds(0, NX * NZ - 1)], o_sem.at[0])
    wait(pr_recv, p_sem.at[0])


def hand_out(a, b, c, out_a, out_b, out_c, sem):
    copies = [
        pltpu.make_async_copy(src, dst, sem.at[i])
        for i, (src, dst) in enumerate(((b, out_b), (c, out_c), (a, out_a)))
    ]
    for copy in copies:
        copy.start()
    for copy in copies:
        copy.wait()


def body(hid, wq, wk, wv, wo, qg, kg, pg, kc, vc, lens, parents, leaf):
    half = np.arange(HEAD_DIM // 2, dtype=np.float32)
    freqs = np.power(np.float32(THETA), np.float32(-2.0) * half / np.float32(HEAD_DIM)).astype(np.float32)
    freq = jnp.asarray(np.concatenate([freqs, freqs])[None])
    vmem, sems = pltpu.VMEM, pltpu.SemaphoreType.DMA
    full = NC * BLOCK
    scratch = [
        vmem(hid.shape, BF16), vmem(wq.shape, BF16), vmem(wk.shape, BF16), vmem(wv.shape, BF16), vmem(wo.shape, BF16),
        vmem((1, WIDTH), F32), vmem((1, WIDTH), F32), vmem((1, WIDTH), F32),
        vmem(parents.shape, jnp.int32), vmem((1, HEAD_DIM), F32),
        pltpu.SMEM(lens.shape, jnp.int32), pltpu.SMEM(leaf.shape, jnp.int32),
        vmem((REQ, full, WIDTH), BF16), vmem((REQ, full, WIDTH), BF16), vmem((REQ, DRAFT, DRAFT), BF16),
        vmem((2, 8, HEAD_DIM), F32), vmem((2, NT - 1, 8, HEAD_DIM), F32),
        vmem((ROWS, HEAD_DIM), BF16), vmem((ROWS, HEAD_DIM), BF16), vmem((ROWS, HEAD_DIM), BF16),
        vmem((NX * NZ, ROWS, HEAD_DIM), BF16),
        vmem((NC, NX, NZ, ROWS, HEAD_DIM), BF16), vmem((NC, NX, NZ, ROWS, HEAD_DIM), BF16),
        vmem((NX, NZ, ROWS, HEAD_DIM), BF16), vmem((NX, 1, 2 * HEAD_DIM), F32),
        vmem((NX * NZ, ROWS, HEAD_DIM), BF16), vmem((NX * NZ, 1, 2 * HEAD_DIM), F32),
        vmem((ROWS, HEAD_DIM), F32), vmem((ROWS, WIDTH), F32),
        vmem((ROWS, WIDTH), BF16), vmem((NT - 1, ROWS, WIDTH), BF16),
        sems((14,)), sems((4,)), sems((4,)), sems((NX,)), sems, sems((4,)), sems((8,)), sems((16,)),
        sems((2,)), sems((2,)), sems((2,)), pltpu.SemaphoreType.REGULAR,
    ]
    anywhere = pl.BlockSpec(memory_space=pltpu.HBM)
    results = pl.pallas_call(
        kernel,
        out_shape=(vmem((OWN, WIDTH), BF16), vmem(kc.shape, BF16), vmem(vc.shape, BF16)),
        in_specs=[anywhere] * 14,
        out_specs=(pl.BlockSpec(memory_space=pltpu.VMEM),) * 3,
        scratch_shapes=scratch,
        compiler_params=pltpu.CompilerParams(
            collective_id=0, has_side_effects=True, vmem_limit_bytes=VMEM1
        ),
        cost_estimate=pl.CostEstimate(flops=300000000, bytes_accessed=11000000, transcendentals=200000),
        name="tree_attention",
    )(*(pltpu.with_memory_space_constraint(part, pltpu.HBM) for part in (
        hid, wq, wk, wv, wo, qg.reshape(1, WIDTH), kg.reshape(1, WIDTH), pg.reshape(1, WIDTH),
        kc, vc, lens, parents, leaf, freq,
    )))
    return pl.pallas_call(
        hand_out,
        out_shape=tuple(jax.ShapeDtypeStruct(part.shape, part.dtype) for part in results),
        in_specs=[pl.BlockSpec(memory_space=pltpu.VMEM)] * 3,
        out_specs=(anywhere,) * 3,
        scratch_shapes=[sems((3,))],
        compiler_params=pltpu.CompilerParams(vmem_limit_bytes=VMEM2),
        cost_estimate=pl.CostEstimate(flops=0, bytes_accessed=2200000, transcendentals=0),
        name="hand_out",
    )(*results)


def solution(mesh):
    return jax.shard_map(
        body,
        mesh=mesh,
        in_specs=(
            P("seq", None),
            P(None, "tp"),
            P(None, "tp"),
            P(None, "tp"),
            P("tp", None),
            P("tp"),
            P("tp"),
            P("tp"),
            P(None, "seq", "tp"),
            P(None, "seq", "tp"),
            P(),
            P(),
            P(),
        ),
        out_specs=(P("seq", "tp"), P(None, "seq", "tp"), P(None, "seq", "tp")),
        check_vma=False,
    )
```

```python
import math

import jax
import jax.numpy as jnp
import numpy as np
from jax import lax
from jax.experimental import pallas as pl
from jax.experimental.pallas import tpu as pltpu
from jax.sharding import PartitionSpec as P

HEAD_DIM = 128
EPS = 1e-06
THETA = 500000.0
NEG = -1e30
NX, NZ, NC, NT = 4, 8, 2, 4
HEADS = 4
OWN = 4
ROWS = HEADS * OWN
DRAFT = 64
REQ = 4
WIDTH = HEADS * HEAD_DIM
BLOCK = 128
MESH = pl.DeviceIdType.MESH
F32 = jnp.float32
BF16 = jnp.bfloat16
VMEM1 = 48 * 1024 * 1024
VMEM2 = 16 * 1024 * 1024
PLANES = (2, 1, 3, 0)
FAR_Z = (4, 3, 5, 2, 6, 1, 7, 0)


def far_first():
    hops = lambda a, b: min(a, NX - a) + min(b, NZ - b)
    pairs = [(a, b) for a in range(NX) for b in range(NZ) if (a, b) != (0, 0)]
    return sorted(pairs, key=lambda pair: -hops(*pair))


def iota(shape, dim):
    return lax.broadcasted_iota(jnp.int32, shape, dim)


def nt_dot(a, b):
    return lax.dot_general(a, b, (((1,), (1,)), ((), ())), preferred_element_type=F32)


def dot(a, b):
    return jnp.dot(a, b, preferred_element_type=F32)


def kernel(
    hid, wq, wk, wv, wo, qg, kg, pg, kc, vc, lens, par, leaf, freq,
    out_h, out_k, out_v,
    hid_s, wq_s, wk_s, wv_s, wo_s, qg_s, kg_s, pg_s, par_s, freq_s, lens_s, leaf_s,
    kfull, vfull, anc_s, sq_send, sq_recv, q_own, k_own, v_own, qbuf, kbuf, vbuf,
    o_st, s_st, obuf, sbuf, att_s, pr_s, pr_send, pr_recv,
    lsem, swap_sem, sq_sem, q_sem, q_send, z_sem, x_sem, c_sem, o_sem, s_sem, p_sem, plane_sem,
):
    seq = lax.axis_index("seq")
    tp = lax.axis_index("tp")
    core = lax.rem(seq, NC)
    zz = lax.rem(seq // NC, NZ)
    xx = seq // (NC * NZ)

    def at(dx, dz, on=core):
        return ((lax.rem(xx + dx, NX) * NZ + lax.rem(zz + dz, NZ)) * NC + on, tp)

    partner = (seq + 1 - 2 * core, tp)
    y_peers = [(seq, lax.rem(tp + d, NT)) for d in range(1, NT)]
    plane_peers = [at(a, b, 1) for a, b in far_first()]
    x_peers = [at(a, 0) for a in range(1, NX)]
    near_peers = [at(0, b) for b in range(1, NZ)] + x_peers + y_peers + [partner]

    barrier = pltpu.get_barrier_semaphore()
    for peer in near_peers:
        pl.semaphore_signal(barrier, inc=1, device_id=peer, device_id_type=MESH)

    @pl.when(core == 1)
    def _():
        for dz in range(1, NZ):
            pl.semaphore_signal(barrier, inc=1, device_id=at(0, dz, 0), device_id_type=MESH)

    pairs = [
        (par, par_s), (hid, hid_s), (wq, wq_s), (lens, lens_s), (freq, freq_s), (qg, qg_s), (kg, kg_s),
        (wk, wk_s), (wv, wv_s), (pg, pg_s), (leaf, leaf_s),
        (kc, kfull.at[:, pl.ds(core * BLOCK, BLOCK), :]),
        (vc, vfull.at[:, pl.ds(core * BLOCK, BLOCK), :]),
        (wo, wo_s),
    ]
    local = [pltpu.make_async_copy(a, b, lsem.at[i]) for i, (a, b) in enumerate(pairs)]
    for copy in local:
        copy.start()
    (c_par, c_hid, c_wq, c_lens, c_freq, c_qg, c_kg, c_wk, c_wv, c_pg, c_leaf, c_kc, c_vc, c_wo) = local

    def remote(src, dst, send, recv, peer):
        copy = pltpu.make_async_remote_copy(
            src_ref=src, dst_ref=dst, send_sem=send, recv_sem=recv, device_id=peer, device_id_type=MESH
        )
        copy.start()

    def wait(ref, sem):
        pltpu.make_async_copy(ref, ref, sem).wait()

    c_par.wait()
    square = (DRAFT, DRAFT)
    eye = (iota(square, 0) == iota(square, 1)).astype(F32)
    chains = []
    for r in range(REQ):
        up = (par_s[pl.ds(r, 1), :] == iota(square, 0)).astype(F32)
        chains.append((eye + up).astype(BF16))
    for _ in range(6):
        chains = [jnp.minimum(dot(a, a), 1.0).astype(BF16) for a in chains]
    for r in range(REQ):
        anc_s[r] = chains[r]

    chunk = (ROWS, HEAD_DIM)
    row_head = (iota(chunk, 0) >> 2) & 3
    lane = iota(chunk, 1)

    def ancestors_of(c):
        row_token = (zz * NC + c) * OWN + (iota((ROWS, DRAFT), 0) & 3)
        one_hot = (iota((ROWS, DRAFT), 1) == row_token).astype(F32).astype(BF16)
        return nt_dot(one_hot, anc_s[xx])

    anc_rows = ancestors_of(core)
    depth = jnp.sum(anc_rows, axis=1, keepdims=True) - 1.0
    c_lens.wait()
    position = lens_s[xx].astype(F32) + depth
    c_freq.wait()
    angle = position * freq_s[...]
    cosine = jnp.cos(angle)
    sine = jnp.sin(angle)
    sine = jnp.where(lane < HEAD_DIM // 2, -sine, sine)

    c_hid.wait()
    h4 = hid_s[...].astype(F32)
    h8 = jnp.concatenate([h4, h4], axis=0)
    h16 = jnp.concatenate([h8, h8], axis=0).astype(BF16)

    def diagonal(wide):
        picked = wide[:, :HEAD_DIM]
        for h in range(1, HEADS):
            picked = jnp.where(row_head == h, wide[:, h * HEAD_DIM : (h + 1) * HEAD_DIM], picked)
        return picked

    def spread(gain):
        return diagonal(jnp.broadcast_to(gain, (ROWS, WIDTH)))

    lane8 = iota((8, HEAD_DIM), 1)

    def turned(wide, gain):
        x = diagonal(wide) * spread(gain)
        return x * cosine + pltpu.roll(x, HEAD_DIM // 2, 1) * sine

    def square_sum(wide):
        return jnp.broadcast_to(jnp.sum(wide * wide, axis=1, keepdims=True)[:8], (8, HEAD_DIM))

    def scaled(x, i):
        wait(sq_recv.at[i], sq_sem.at[2 * i + 1])
        total = sq_send[i] + sq_recv[i, 0] + sq_recv[i, 1] + sq_recv[i, 2]
        scale = lax.rsqrt(total / (NT * WIDTH) + EPS)
        return (x * jnp.concatenate([scale, scale], axis=0)).astype(BF16)

    c_wq.wait()
    q_wide = dot(h16, wq_s[...])
    sq_send[0] = square_sum(q_wide)

    pl.semaphore_wait(barrier, len(near_peers) + (NZ - 1) * (1 - core))
    for i, peer in enumerate(y_peers):
        remote(sq_send.at[0], sq_recv.at[0, i], sq_sem.at[0], sq_sem.at[1], peer)
    for peer in x_peers:
        pl.semaphore_signal(plane_sem, inc=1, device_id=peer, device_id_type=MESH)

    for copy in (c_qg, c_kg):
        copy.wait()
    q_turn = turned(q_wide, qg_s[...])
    c_wk.wait()
    k_wide = dot(h16, wk_s[...])
    sq_send[1] = square_sum(k_wide)
    for i, peer in enumerate(y_peers):
        remote(sq_send.at[1], sq_recv.at[1, i], sq_sem.at[2], sq_sem.at[3], peer)
    mine = pl.ds(core * BLOCK, BLOCK)
    first_block = pl.ds(0, BLOCK)

    @pl.when(core == 0)
    def _():
        remote(kc, kfull.at[:, first_block, :], swap_sem.at[0], swap_sem.at[1], partner)
        remote(vc, vfull.at[:, first_block, :], swap_sem.at[2], swap_sem.at[3], partner)

    k_turn = turned(k_wide, kg_s[...])
    c_wv.wait()
    v_own[...] = diagonal(dot(h16, wv_s[...])).astype(BF16)
    for dz in FAR_Z[:-1]:
        remote(v_own, vbuf.at[core, xx, zz], z_sem.at[2], z_sem.at[3], at(0, dz))
    pltpu.make_async_copy(v_own, vbuf.at[core, xx, zz], z_sem.at[3]).start()

    q_own[...] = scaled(q_turn, 0)
    pl.semaphore_wait(plane_sem, len(x_peers))

    slot = xx * NZ + zz
    q_ready = q_sem.at[core * NX + xx]
    for peer in plane_peers:
        remote(q_own, qbuf.at[core * NX * NZ + slot], q_send, q_ready, peer)

    @pl.when(core == 0)
    def _():
        remote(q_own, qbuf.at[slot], q_send, q_ready, partner)

    @pl.when(core == 1)
    def _():
        pltpu.make_async_copy(q_own, qbuf.at[NX * NZ + slot], q_ready).start()

    k_own[...] = scaled(k_turn, 1)
    for dz in FAR_Z[:-1]:
        remote(k_own, kbuf.at[core, xx, zz], z_sem.at[0], z_sem.at[1], at(0, dz))
    pltpu.make_async_copy(k_own, kbuf.at[core, xx, zz], z_sem.at[1]).start()

    def onward(buf, sem, first, at_x, at_c):
        wait(buf.at[core, xx], z_sem.at[sem])
        for far in (2, 1, 3):
            remote(buf.at[core, xx], buf.at[core, xx], x_sem.at[first], x_sem.at[at_x + far], at(far, 0))
        remote(buf.at[core, xx], buf.at[core, xx], c_sem.at[at_c], c_sem.at[at_c + 1], partner)

    factor = 1.0 / math.sqrt(HEAD_DIM)
    c_kc.wait()
    c_vc.wait()

    @pl.when(core == 0)
    def _():
        onward(vbuf, 3, 1, 4, 2)
        onward(kbuf, 1, 0, 1, 0)

    @pl.when(core == 1)
    def _():
        tall = (NZ * ROWS, NC * BLOCK)
        tall_head = (iota(tall, 0) >> 2) & 3
        place = (seq - 1) * BLOCK + iota(tall, 1)
        turn = iota((NZ * ROWS, HEAD_DIM), 0) == iota((NZ * ROWS, HEAD_DIM), 1)
        onward(vbuf, 3, 1, 4, 2)
        wait(kfull.at[:, first_block, :], swap_sem.at[1])
        wait(vfull.at[:, first_block, :], swap_sem.at[3])
        for step, (c, dx) in enumerate([(c, dx) for c in (1, 0) for dx in PLANES]):
            if step == 2:
                onward(kbuf, 1, 0, 1, 0)
            r = lax.rem(xx + dx, NX)
            group = pl.ds((c * NX + r) * NZ, NZ)
            wait(qbuf.at[group], q_sem.at[c * NX + r])
            queries = qbuf[group].reshape(NZ * ROWS, HEAD_DIM)
            scores = None
            for h in range(HEADS):
                part = nt_dot(queries, kfull[r, :, h * HEAD_DIM : (h + 1) * HEAD_DIM])
                scores = part if h == 0 else jnp.where(tall_head == h, part, scores)
            visible = place < lens_s[r]
            scores = jnp.where(visible, scores * factor, NEG)
            peak = jnp.max(scores, axis=1, keepdims=True)
            weights = jnp.where(visible, jnp.exp(scores - peak), 0.0)
            weight_sum = jnp.sum(weights, axis=1, keepdims=True)
            mixed = None
            for h in range(HEADS):
                masked = jnp.where(tall_head == h, weights, 0.0).astype(BF16)
                part = dot(masked, vfull[r, :, h * HEAD_DIM : (h + 1) * HEAD_DIM])
                mixed = part if h == 0 else mixed + part
            o_st[step] = mixed.astype(BF16).reshape(NZ, ROWS, HEAD_DIM)
            s_st[step, :, :HEAD_DIM] = jnp.sum(jnp.where(turn, peak, 0.0), axis=0, keepdims=True)
            s_st[step, :, HEAD_DIM:] = jnp.sum(jnp.where(turn, weight_sum, 0.0), axis=0, keepdims=True)
            there = c * NX * NZ + slot
            for dz in FAR_Z:
                to = lax.rem(zz + dz, NZ)
                if (dx, dz) == (0, 0):
                    pltpu.make_async_copy(o_st.at[step, to], obuf.at[there], o_sem.at[1 + c]).start()
                    pltpu.make_async_copy(s_st.at[step], sbuf.at[there], s_sem.at[1 + c]).start()
                else:
                    remote(s_st.at[step], sbuf.at[there], s_sem.at[0], s_sem.at[1 + c], at(dx, dz))
                    remote(o_st.at[step, to], obuf.at[there], o_sem.at[0], o_sem.at[1 + c], at(dx, dz))

    wait(kbuf.at[core, xx], c_sem.at[1])
    wait(vbuf.at[core, xx], c_sem.at[3])
    both = NC * NZ * ROWS
    col = iota((DRAFT, both), 1)
    col_token = ((col >> 4) & 7) * (NC * OWN) + (col >> 7) * OWN + (col & 3)
    expand = (iota((DRAFT, both), 0) == col_token).astype(F32).astype(BF16)

    def request_rows(buf, r):
        return jnp.concatenate([buf[c, r].reshape(NZ * ROWS, HEAD_DIM) for c in range(NC)], axis=0)

    for i, dx in enumerate((1, 3, 2)):
        r = lax.rem(xx + dx, NX)
        wait(kbuf.at[core, r], x_sem.at[1 + (NX - dx)])
        wait(vbuf.at[core, r], x_sem.at[4 + (NX - dx)])
        remote(kbuf.at[core, r], kbuf.at[core, r], c_sem.at[4 + 4 * i], c_sem.at[5 + 4 * i], partner)
        remote(vbuf.at[core, r], vbuf.at[core, r], c_sem.at[6 + 4 * i], c_sem.at[7 + 4 * i], partner)

    c_leaf.wait()
    p_place = (seq * BLOCK + iota((BLOCK, DRAFT), 0)).astype(F32)
    col_head = (iota((BLOCK, both), 1) >> 2) & 3

    def compact(i, dx):
        r = lax.rem(xx + dx, NX)
        if dx:
            wait(kbuf.at[core, r], c_sem.at[1 + 4 * i])
            wait(vbuf.at[core, r], c_sem.at[3 + 4 * i])
        anc = anc_s[r]
        target = jnp.sum(anc.astype(F32), axis=0, keepdims=True) - 1.0 + lens_s[r].astype(F32)
        leaf_hot = (iota((ROWS, DRAFT), 1) == leaf_s[r]).astype(F32).astype(BF16)
        on_path = nt_dot(leaf_hot, anc)[:1]
        placing = jnp.where((p_place == target) & (on_path > 0.5), 1.0, 0.0)
        written = jnp.sum(placing, axis=1, keepdims=True) > 0.5
        placing = dot(placing.astype(BF16), expand)
        k_rows = request_rows(kbuf, r)
        v_rows = request_rows(vbuf, r)
        for h in range(HEADS):
            columns = slice(h * HEAD_DIM, (h + 1) * HEAD_DIM)
            pick = jnp.where(col_head == h, placing, 0.0).astype(BF16)
            old_k = kfull[r, mine, columns].astype(F32)
            old_v = vfull[r, mine, columns].astype(F32)
            out_k[r, :, columns] = jnp.where(written, dot(pick, k_rows), old_k).astype(BF16)
            out_v[r, :, columns] = jnp.where(written, dot(pick, v_rows), old_v).astype(BF16)

    compact(0, 0)

    @pl.when(core == 1)
    def _():
        wide_shape = (ROWS, both)
        same_head = ((iota(wide_shape, 1) >> 2) & 3) == ((iota(wide_shape, 0) >> 2) & 3)
        here = lane == zz * ROWS + iota(chunk, 0)

        def column(row):
            return jnp.sum(jnp.where(here, row, 0.0), axis=1, keepdims=True)

        drafts = []
        for c in (1, 0):
            allowed = (dot(ancestors_of(c).astype(BF16), expand) > 0.5) & same_head
            d_scores = nt_dot(qbuf[c * NX * NZ + slot], request_rows(kbuf, xx)) * factor
            d_scores = jnp.where(allowed, d_scores, NEG)
            d_peak = jnp.max(d_scores, axis=1, keepdims=True)
            d_weights = jnp.where(allowed, jnp.exp(d_scores - d_peak), 0.0)
            d_sum = jnp.sum(d_weights, axis=1, keepdims=True)
            drafts.append((c, d_peak, d_sum, dot(d_weights.astype(BF16), request_rows(vbuf, xx))))
        for c, d_peak, d_sum, d_out in drafts:
            base = c * NX * NZ
            arrived = pl.ds(base, NX * NZ)
            wait(sbuf.at[arrived], s_sem.at[1 + c])
            wait(obuf.at[arrived], o_sem.at[1 + c])
            peaks = sbuf[arrived, :, :HEAD_DIM]
            highest = jnp.max(peaks, axis=0)
            shares = jnp.exp(peaks - highest[None])
            sums = jnp.sum(shares * sbuf[arrived, :, HEAD_DIM:], axis=0)
            top = column(highest)
            merged = None
            for s in range(NX * NZ):
                part = column(shares[s]) * obuf[base + s].astype(F32)
                merged = part if s == 0 else merged + part
            best = jnp.maximum(top, d_peak)
            c_share = jnp.exp(top - best)
            d_share = jnp.exp(d_peak - best)
            att_s[...] = (merged * c_share + d_out * d_share) / (column(sums) * c_share + d_sum * d_share)
            att4 = [att_s[h * OWN : (h + 1) * OWN, :] for h in range(HEADS)]
            att4 = jnp.concatenate(att4, axis=1).astype(BF16)
            if c == 1:
                c_wo.wait()
            for n in range(NT):
                pr_s[n * OWN : (n + 1) * OWN, :] = dot(att4, wo_s[:, n * WIDTH : (n + 1) * WIDTH])
            pr_send[c] = pr_s[...].astype(BF16)
            for i, peer in enumerate(y_peers):
                remote(pr_send.at[c], pr_recv.at[i], p_sem.at[2 * c], p_sem.at[1], (peer[0] - 1 + c, peer[1]))
            if c == 0:
                remote(pr_send.at[0], pr_recv.at[NT - 1], p_sem.at[0], p_sem.at[1], partner)
            else:
                pr_recv[NT - 1] = pr_send[1]

    @pl.when(core == 0)
    def _():
        c_wo.wait()

    for i, dx in enumerate((1, 3, 2)):
        compact(i + 1, dx)
    c_pg.wait()

    @pl.when(core == 0)
    def _():
        wait(pr_recv, p_sem.at[1])

    @pl.when(core == 1)
    def _():
        wait(pr_recv.at[pl.ds(0, NT - 1)], p_sem.at[1])

    whole = pr_recv[0].astype(F32) + pr_recv[1].astype(F32) + pr_recv[2].astype(F32) + pr_recv[3].astype(F32)
    pr_s[...] = whole
    quarters = [pr_s[n * OWN : (n + 1) * OWN, :] for n in range(NT)]
    squares = sum(part * part for part in quarters)
    power = jnp.sum(squares, axis=1, keepdims=True)
    own = quarters[0]
    for n in range(1, NT):
        own = jnp.where(tp == n, quarters[n], own)
    normed = own * lax.rsqrt(power / (NT * WIDTH) + EPS) * pg_s[...]
    residual = hid_s[:, pl.ds(pl.multiple_of(tp * WIDTH, WIDTH), WIDTH)].astype(F32)
    out_h[...] = (residual + normed).astype(BF16)

    wait(sq_recv.at[0], sq_sem.at[0])
    wait(sq_recv.at[1], sq_sem.at[2])
    @pl.when(core == 0)
    def _():
        wait(kfull.at[:, first_block, :], swap_sem.at[0])
        wait(vfull.at[:, first_block, :], swap_sem.at[2])
        wait(qbuf.at[pl.ds(0, NX * NZ)], q_send)

    @pl.when(core == 1)
    def _():
        wait(qbuf.at[pl.ds(0, NX * NZ - 1)], q_send)
        wait(sbuf.at[pl.ds(0, 2 * (NX * NZ - 1))], s_sem.at[0])
        wait(obuf.at[pl.ds(0, 2 * (NX * NZ - 1))], o_sem.at[0])
        wait(pr_recv, p_sem.at[0])
        wait(pr_recv.at[pl.ds(0, NT - 1)], p_sem.at[2])

    wait(kbuf.at[0, 0, pl.ds(0, NZ - 1)], z_sem.at[0])
    wait(vbuf.at[0, 0, pl.ds(0, NZ - 1)], z_sem.at[2])
    wait(kbuf.at[0, pl.ds(0, NX - 1)], x_sem.at[0])
    wait(vbuf.at[0, pl.ds(0, NX - 1)], x_sem.at[1])
    for i in range(NX):
        wait(kbuf.at[0, 0], c_sem.at[4 * i])
        wait(vbuf.at[0, 0], c_sem.at[4 * i + 2])


def hand_out(a, b, c, out_a, out_b, out_c, sem):
    copies = [
        pltpu.make_async_copy(src, dst, sem.at[i])
        for i, (src, dst) in enumerate(((b, out_b), (c, out_c), (a, out_a)))
    ]
    for copy in copies:
        copy.start()
    for copy in copies:
        copy.wait()


def body(hid, wq, wk, wv, wo, qg, kg, pg, kc, vc, lens, parents, leaf):
    half = np.arange(HEAD_DIM // 2, dtype=np.float32)
    freqs = np.power(np.float32(THETA), np.float32(-2.0) * half / np.float32(HEAD_DIM)).astype(np.float32)
    freq = jnp.asarray(np.concatenate([freqs, freqs])[None])
    vmem, sems = pltpu.VMEM, pltpu.SemaphoreType.DMA
    full = NC * BLOCK
    scratch = [
        vmem(hid.shape, BF16), vmem(wq.shape, BF16), vmem(wk.shape, BF16), vmem(wv.shape, BF16), vmem(wo.shape, BF16),
        vmem((1, WIDTH), F32), vmem((1, WIDTH), F32), vmem((1, WIDTH), F32),
        vmem(parents.shape, jnp.int32), vmem((1, HEAD_DIM), F32),
        pltpu.SMEM(lens.shape, jnp.int32), pltpu.SMEM(leaf.shape, jnp.int32),
        vmem((REQ, full, WIDTH), BF16), vmem((REQ, full, WIDTH), BF16), vmem((REQ, DRAFT, DRAFT), BF16),
        vmem((2, 8, HEAD_DIM), F32), vmem((2, NT - 1, 8, HEAD_DIM), F32),
        vmem((ROWS, HEAD_DIM), BF16), vmem((ROWS, HEAD_DIM), BF16), vmem((ROWS, HEAD_DIM), BF16),
        vmem((NC * NX * NZ, ROWS, HEAD_DIM), BF16),
        vmem((NC, NX, NZ, ROWS, HEAD_DIM), BF16), vmem((NC, NX, NZ, ROWS, HEAD_DIM), BF16),
        vmem((NC * NX, NZ, ROWS, HEAD_DIM), BF16), vmem((NC * NX, 1, 2 * HEAD_DIM), F32),
        vmem((NC * NX * NZ, ROWS, HEAD_DIM), BF16), vmem((NC * NX * NZ, 1, 2 * HEAD_DIM), F32),
        vmem((ROWS, HEAD_DIM), F32), vmem((ROWS, WIDTH), F32),
        vmem((NC, ROWS, WIDTH), BF16), vmem((NT, ROWS, WIDTH), BF16),
        sems((14,)), sems((4,)), sems((4,)), sems((NC * NX,)), sems, sems((4,)), sems((8,)), sems((16,)),
        sems((3,)), sems((3,)), sems((3,)), pltpu.SemaphoreType.REGULAR,
    ]
    anywhere = pl.BlockSpec(memory_space=pltpu.HBM)
    results = pl.pallas_call(
        kernel,
        out_shape=(vmem((OWN, WIDTH), BF16), vmem(kc.shape, BF16), vmem(vc.shape, BF16)),
        in_specs=[anywhere] * 14,
        out_specs=(pl.BlockSpec(memory_space=pltpu.VMEM),) * 3,
        scratch_shapes=scratch,
        compiler_params=pltpu.CompilerParams(
            collective_id=0, has_side_effects=True, vmem_limit_bytes=VMEM1
        ),
        cost_estimate=pl.CostEstimate(flops=300000000, bytes_accessed=11000000, transcendentals=200000),
        name="tree_attention",
    )(*(pltpu.with_memory_space_constraint(part, pltpu.HBM) for part in (
        hid, wq, wk, wv, wo, qg.reshape(1, WIDTH), kg.reshape(1, WIDTH), pg.reshape(1, WIDTH),
        kc, vc, lens, parents, leaf, freq,
    )))
    return pl.pallas_call(
        hand_out,
        out_shape=tuple(jax.ShapeDtypeStruct(part.shape, part.dtype) for part in results),
        in_specs=[pl.BlockSpec(memory_space=pltpu.VMEM)] * 3,
        out_specs=(anywhere,) * 3,
        scratch_shapes=[sems((3,))],
        compiler_params=pltpu.CompilerParams(vmem_limit_bytes=VMEM2),
        cost_estimate=pl.CostEstimate(flops=0, bytes_accessed=2200000, transcendentals=0),
        name="hand_out",
    )(*results)


def solution(mesh):
    return jax.shard_map(
        body,
        mesh=mesh,
        in_specs=(
            P("seq", None),
            P(None, "tp"),
            P(None, "tp"),
            P(None, "tp"),
            P("tp", None),
            P("tp"),
            P("tp"),
            P("tp"),
            P(None, "seq", "tp"),
            P(None, "seq", "tp"),
            P(),
            P(),
            P(),
        ),
        out_specs=(P("seq", "tp"), P(None, "seq", "tp"), P(None, "seq", "tp")),
        check_vma=False,
    )
```

```python
import math

import jax
import jax.numpy as jnp
import numpy as np
from jax import lax
from jax.experimental import pallas as pl
from jax.experimental.pallas import tpu as pltpu
from jax.sharding import PartitionSpec as P

HEAD_DIM = 128
EPS = 1e-06
THETA = 500000.0
NEG = -1e30
NX, NZ, NC, NT = 4, 8, 2, 4
HEADS = 4
OWN = 4
ROWS = HEADS * OWN
DRAFT = 64
REQ = 4
WIDTH = HEADS * HEAD_DIM
BLOCK = 128
MESH = pl.DeviceIdType.MESH
F32 = jnp.float32
BF16 = jnp.bfloat16
VMEM1 = 48 * 1024 * 1024
VMEM2 = 16 * 1024 * 1024
PLANES = (2, 1, 3, 0)
FAR_Z = (4, 3, 5, 2, 6, 1, 7, 0)


def far_first():
    hops = lambda a, b: min(a, NX - a) + min(b, NZ - b)
    pairs = [(a, b) for a in range(NX) for b in range(NZ) if (a, b) != (0, 0)]
    return sorted(pairs, key=lambda pair: -hops(*pair))


def iota(shape, dim):
    return lax.broadcasted_iota(jnp.int32, shape, dim)


def nt_dot(a, b):
    return lax.dot_general(a, b, (((1,), (1,)), ((), ())), preferred_element_type=F32)


def dot(a, b):
    return jnp.dot(a, b, preferred_element_type=F32)


def kernel(
    hid, wq, wk, wv, wo, qg, kg, pg, kc, vc, lens, par, leaf, freq,
    out_h, out_k, out_v,
    hid_s, wq_s, wk_s, wv_s, wo_s, qg_s, kg_s, pg_s, par_s, freq_s, lens_s, leaf_s,
    kfull, vfull, anc_s, sq_send, sq_recv, q_own, k_own, v_own, qbuf, kbuf, vbuf,
    o_st, s_st, obuf, sbuf, att_s, pr_s, pr_send, pr_recv,
    lsem, swap_sem, sq_sem, q_sem, q_send, z_sem, x_sem, c_sem, o_sem, s_sem, p_sem, plane_sem,
):
    seq = lax.axis_index("seq")
    tp = lax.axis_index("tp")
    core = lax.rem(seq, NC)
    zz = lax.rem(seq // NC, NZ)
    xx = seq // (NC * NZ)

    def at(dx, dz, on=core):
        return ((lax.rem(xx + dx, NX) * NZ + lax.rem(zz + dz, NZ)) * NC + on, tp)

    partner = (seq + 1 - 2 * core, tp)
    y_peers = [(seq, lax.rem(tp + d, NT)) for d in range(1, NT)]
    plane_peers = [at(a, b, 1) for a, b in far_first()]
    x_peers = [at(a, 0) for a in range(1, NX)]
    near_peers = [at(0, b) for b in range(1, NZ)] + x_peers + y_peers + [partner]

    barrier = pltpu.get_barrier_semaphore()
    for peer in near_peers:
        pl.semaphore_signal(barrier, inc=1, device_id=peer, device_id_type=MESH)

    @pl.when(core == 1)
    def _():
        for dz in range(1, NZ):
            pl.semaphore_signal(barrier, inc=1, device_id=at(0, dz, 0), device_id_type=MESH)

    pairs = [
        (par, par_s), (hid, hid_s), (wq, wq_s), (lens, lens_s), (freq, freq_s), (qg, qg_s), (kg, kg_s),
        (wk, wk_s), (wv, wv_s), (pg, pg_s), (leaf, leaf_s),
        (kc, kfull.at[:, pl.ds(core * BLOCK, BLOCK), :]),
        (vc, vfull.at[:, pl.ds(core * BLOCK, BLOCK), :]),
        (wo, wo_s),
    ]
    local = [pltpu.make_async_copy(a, b, lsem.at[i]) for i, (a, b) in enumerate(pairs)]
    for copy in local:
        copy.start()
    (c_par, c_hid, c_wq, c_lens, c_freq, c_qg, c_kg, c_wk, c_wv, c_pg, c_leaf, c_kc, c_vc, c_wo) = local

    def remote(src, dst, send, recv, peer):
        copy = pltpu.make_async_remote_copy(
            src_ref=src, dst_ref=dst, send_sem=send, recv_sem=recv, device_id=peer, device_id_type=MESH
        )
        copy.start()

    def wait(ref, sem):
        pltpu.make_async_copy(ref, ref, sem).wait()

    c_par.wait()
    square = (DRAFT, DRAFT)
    eye = (iota(square, 0) == iota(square, 1)).astype(F32)
    chains = []
    for r in range(REQ):
        up = (par_s[pl.ds(r, 1), :] == iota(square, 0)).astype(F32)
        chains.append((eye + up).astype(BF16))
    for _ in range(6):
        chains = [jnp.minimum(dot(a, a), 1.0).astype(BF16) for a in chains]
    for r in range(REQ):
        anc_s[r] = chains[r]

    chunk = (ROWS, HEAD_DIM)
    row_head = (iota(chunk, 0) >> 2) & 3
    lane = iota(chunk, 1)

    def ancestors_of(c):
        row_token = (zz * NC + c) * OWN + (iota((ROWS, DRAFT), 0) & 3)
        one_hot = (iota((ROWS, DRAFT), 1) == row_token).astype(F32).astype(BF16)
        return nt_dot(one_hot, anc_s[xx])

    anc_rows = ancestors_of(core)
    depth = jnp.sum(anc_rows, axis=1, keepdims=True) - 1.0
    c_lens.wait()
    position = lens_s[xx].astype(F32) + depth
    c_freq.wait()
    angle = position * freq_s[...]
    cosine = jnp.cos(angle)
    sine = jnp.sin(angle)
    sine = jnp.where(lane < HEAD_DIM // 2, -sine, sine)

    c_hid.wait()
    h4 = hid_s[...].astype(F32)
    h8 = jnp.concatenate([h4, h4], axis=0)
    h16 = jnp.concatenate([h8, h8], axis=0).astype(BF16)

    def diagonal(wide):
        picked = wide[:, :HEAD_DIM]
        for h in range(1, HEADS):
            picked = jnp.where(row_head == h, wide[:, h * HEAD_DIM : (h + 1) * HEAD_DIM], picked)
        return picked

    def spread(gain):
        return diagonal(jnp.broadcast_to(gain, (ROWS, WIDTH)))

    lane8 = iota((8, HEAD_DIM), 1)

    def turned(wide, gain):
        x = diagonal(wide) * spread(gain)
        return x * cosine + pltpu.roll(x, HEAD_DIM // 2, 1) * sine

    def square_sum(wide):
        return jnp.broadcast_to(jnp.sum(wide * wide, axis=1, keepdims=True)[:8], (8, HEAD_DIM))

    def scaled(x, i):
        wait(sq_recv.at[i], sq_sem.at[2 * i + 1])
        total = sq_send[i] + sq_recv[i, 0] + sq_recv[i, 1] + sq_recv[i, 2]
        scale = lax.rsqrt(total / (NT * WIDTH) + EPS)
        return (x * jnp.concatenate([scale, scale], axis=0)).astype(BF16)

    c_wq.wait()
    q_wide = dot(h16, wq_s[...])
    sq_send[0] = square_sum(q_wide)

    pl.semaphore_wait(barrier, len(near_peers) + (NZ - 1) * (1 - core))
    for i, peer in enumerate(y_peers):
        remote(sq_send.at[0], sq_recv.at[0, i], sq_sem.at[0], sq_sem.at[1], peer)
    for peer in x_peers:
        pl.semaphore_signal(plane_sem, inc=1, device_id=peer, device_id_type=MESH)

    for copy in (c_qg, c_kg):
        copy.wait()
    q_turn = turned(q_wide, qg_s[...])
    c_wk.wait()
    k_wide = dot(h16, wk_s[...])
    sq_send[1] = square_sum(k_wide)
    for i, peer in enumerate(y_peers):
        remote(sq_send.at[1], sq_recv.at[1, i], sq_sem.at[2], sq_sem.at[3], peer)
    mine = pl.ds(core * BLOCK, BLOCK)
    first_block = pl.ds(0, BLOCK)

    @pl.when(core == 0)
    def _():
        remote(kc, kfull.at[:, first_block, :], swap_sem.at[0], swap_sem.at[1], partner)
        remote(vc, vfull.at[:, first_block, :], swap_sem.at[2], swap_sem.at[3], partner)

    k_turn = turned(k_wide, kg_s[...])
    c_wv.wait()
    v_own[...] = diagonal(dot(h16, wv_s[...])).astype(BF16)
    for dz in FAR_Z[:-1]:
        remote(v_own, vbuf.at[core, xx, zz], z_sem.at[2], z_sem.at[3], at(0, dz))
    pltpu.make_async_copy(v_own, vbuf.at[core, xx, zz], z_sem.at[3]).start()

    q_own[...] = scaled(q_turn, 0)
    pl.semaphore_wait(plane_sem, len(x_peers))

    slot = xx * NZ + zz
    q_ready = q_sem.at[core * NX + xx]
    for peer in plane_peers:
        remote(q_own, qbuf.at[core * NX * NZ + slot], q_send, q_ready, peer)

    @pl.when(core == 0)
    def _():
        remote(q_own, qbuf.at[slot], q_send, q_ready, partner)

    @pl.when(core == 1)
    def _():
        pltpu.make_async_copy(q_own, qbuf.at[NX * NZ + slot], q_ready).start()

    k_own[...] = scaled(k_turn, 1)
    for dz in FAR_Z[:-1]:
        remote(k_own, kbuf.at[core, xx, zz], z_sem.at[0], z_sem.at[1], at(0, dz))
    pltpu.make_async_copy(k_own, kbuf.at[core, xx, zz], z_sem.at[1]).start()

    def onward(buf, sem, first, at_x, at_c):
        wait(buf.at[core, xx], z_sem.at[sem])
        for far in (2, 1, 3):
            remote(buf.at[core, xx], buf.at[core, xx], x_sem.at[first], x_sem.at[at_x + far], at(far, 0))
        remote(buf.at[core, xx], buf.at[core, xx], c_sem.at[at_c], c_sem.at[at_c + 1], partner)

    factor = 1.0 / math.sqrt(HEAD_DIM)
    c_kc.wait()
    c_vc.wait()

    @pl.when(core == 0)
    def _():
        onward(vbuf, 3, 1, 4, 2)
        onward(kbuf, 1, 0, 1, 0)

    @pl.when(core == 1)
    def _():
        tall = (NZ * ROWS, NC * BLOCK)
        tall_head = (iota(tall, 0) >> 2) & 3
        place = (seq - 1) * BLOCK + iota(tall, 1)
        turn = iota((NZ * ROWS, HEAD_DIM), 0) == iota((NZ * ROWS, HEAD_DIM), 1)
        onward(vbuf, 3, 1, 4, 2)
        wait(kfull.at[:, first_block, :], swap_sem.at[1])
        wait(vfull.at[:, first_block, :], swap_sem.at[3])
        for step, (c, dx) in enumerate([(1, 0), (1, 1), (1, 3), (1, 2), (0, 2), (0, 1), (0, 3), (0, 0)]):
            if step == 2:
                onward(kbuf, 1, 0, 1, 0)
            r = lax.rem(xx + dx, NX)
            group = pl.ds((c * NX + r) * NZ, NZ)
            wait(qbuf.at[group], q_sem.at[c * NX + r])
            queries = qbuf[group].reshape(NZ * ROWS, HEAD_DIM)
            scores = None
            for h in range(HEADS):
                part = nt_dot(queries, kfull[r, :, h * HEAD_DIM : (h + 1) * HEAD_DIM])
                scores = part if h == 0 else jnp.where(tall_head == h, part, scores)
            visible = place < lens_s[r]
            scores = jnp.where(visible, scores * factor, NEG)
            peak = jnp.max(scores, axis=1, keepdims=True)
            weights = jnp.where(visible, jnp.exp(scores - peak), 0.0)
            weight_sum = jnp.sum(weights, axis=1, keepdims=True)
            mixed = None
            for h in range(HEADS):
                masked = jnp.where(tall_head == h, weights, 0.0).astype(BF16)
                part = dot(masked, vfull[r, :, h * HEAD_DIM : (h + 1) * HEAD_DIM])
                mixed = part if h == 0 else mixed + part
            o_st[step] = mixed.astype(BF16).reshape(NZ, ROWS, HEAD_DIM)
            s_st[step, :, :HEAD_DIM] = jnp.sum(jnp.where(turn, peak, 0.0), axis=0, keepdims=True)
            s_st[step, :, HEAD_DIM:] = jnp.sum(jnp.where(turn, weight_sum, 0.0), axis=0, keepdims=True)
            there = c * NX * NZ + slot
            for dz in FAR_Z:
                to = lax.rem(zz + dz, NZ)
                if (dx, dz) == (0, 0):
                    pltpu.make_async_copy(o_st.at[step, to], obuf.at[there], o_sem.at[1 + c]).start()
                    pltpu.make_async_copy(s_st.at[step], sbuf.at[there], s_sem.at[1 + c]).start()
                else:
                    remote(s_st.at[step], sbuf.at[there], s_sem.at[0], s_sem.at[1 + c], at(dx, dz))
                    remote(o_st.at[step, to], obuf.at[there], o_sem.at[0], o_sem.at[1 + c], at(dx, dz))

    wait(kbuf.at[core, xx], c_sem.at[1])
    wait(vbuf.at[core, xx], c_sem.at[3])
    both = NC * NZ * ROWS
    col = iota((DRAFT, both), 1)
    col_token = ((col >> 4) & 7) * (NC * OWN) + (col >> 7) * OWN + (col & 3)
    expand = (iota((DRAFT, both), 0) == col_token).astype(F32).astype(BF16)

    def request_rows(buf, r):
        return jnp.concatenate([buf[c, r].reshape(NZ * ROWS, HEAD_DIM) for c in range(NC)], axis=0)

    for i, dx in enumerate((1, 3, 2)):
        r = lax.rem(xx + dx, NX)
        wait(kbuf.at[core, r], x_sem.at[1 + (NX - dx)])
        wait(vbuf.at[core, r], x_sem.at[4 + (NX - dx)])
        remote(kbuf.at[core, r], kbuf.at[core, r], c_sem.at[4 + 4 * i], c_sem.at[5 + 4 * i], partner)
        remote(vbuf.at[core, r], vbuf.at[core, r], c_sem.at[6 + 4 * i], c_sem.at[7 + 4 * i], partner)

    c_leaf.wait()
    p_place = (seq * BLOCK + iota((BLOCK, DRAFT), 0)).astype(F32)
    col_head = (iota((BLOCK, both), 1) >> 2) & 3

    def compact(i, dx):
        r = lax.rem(xx + dx, NX)
        if dx:
            wait(kbuf.at[core, r], c_sem.at[1 + 4 * i])
            wait(vbuf.at[core, r], c_sem.at[3 + 4 * i])
        anc = anc_s[r]
        target = jnp.sum(anc.astype(F32), axis=0, keepdims=True) - 1.0 + lens_s[r].astype(F32)
        leaf_hot = (iota((ROWS, DRAFT), 1) == leaf_s[r]).astype(F32).astype(BF16)
        on_path = nt_dot(leaf_hot, anc)[:1]
        placing = jnp.where((p_place == target) & (on_path > 0.5), 1.0, 0.0)
        written = jnp.sum(placing, axis=1, keepdims=True) > 0.5
        placing = dot(placing.astype(BF16), expand)
        k_rows = request_rows(kbuf, r)
        v_rows = request_rows(vbuf, r)
        for h in range(HEADS):
            columns = slice(h * HEAD_DIM, (h + 1) * HEAD_DIM)
            pick = jnp.where(col_head == h, placing, 0.0).astype(BF16)
            old_k = kfull[r, mine, columns].astype(F32)
            old_v = vfull[r, mine, columns].astype(F32)
            out_k[r, :, columns] = jnp.where(written, dot(pick, k_rows), old_k).astype(BF16)
            out_v[r, :, columns] = jnp.where(written, dot(pick, v_rows), old_v).astype(BF16)

    compact(0, 0)

    @pl.when(core == 1)
    def _():
        wide_shape = (ROWS, both)
        same_head = ((iota(wide_shape, 1) >> 2) & 3) == ((iota(wide_shape, 0) >> 2) & 3)
        here = lane == zz * ROWS + iota(chunk, 0)

        def column(row):
            return jnp.sum(jnp.where(here, row, 0.0), axis=1, keepdims=True)

        drafts = []
        for c in (1, 0):
            allowed = (dot(ancestors_of(c).astype(BF16), expand) > 0.5) & same_head
            d_scores = nt_dot(qbuf[c * NX * NZ + slot], request_rows(kbuf, xx)) * factor
            d_scores = jnp.where(allowed, d_scores, NEG)
            d_peak = jnp.max(d_scores, axis=1, keepdims=True)
            d_weights = jnp.where(allowed, jnp.exp(d_scores - d_peak), 0.0)
            d_sum = jnp.sum(d_weights, axis=1, keepdims=True)
            drafts.append((c, d_peak, d_sum, dot(d_weights.astype(BF16), request_rows(vbuf, xx))))
        for c, d_peak, d_sum, d_out in drafts:
            base = c * NX * NZ
            arrived = pl.ds(base, NX * NZ)
            wait(sbuf.at[arrived], s_sem.at[1 + c])
            wait(obuf.at[arrived], o_sem.at[1 + c])
            peaks = sbuf[arrived, :, :HEAD_DIM]
            highest = jnp.max(peaks, axis=0)
            shares = jnp.exp(peaks - highest[None])
            sums = jnp.sum(shares * sbuf[arrived, :, HEAD_DIM:], axis=0)
            top = column(highest)
            merged = None
            for s in range(NX * NZ):
                part = column(shares[s]) * obuf[base + s].astype(F32)
                merged = part if s == 0 else merged + part
            best = jnp.maximum(top, d_peak)
            c_share = jnp.exp(top - best)
            d_share = jnp.exp(d_peak - best)
            att_s[...] = (merged * c_share + d_out * d_share) / (column(sums) * c_share + d_sum * d_share)
            att4 = [att_s[h * OWN : (h + 1) * OWN, :] for h in range(HEADS)]
            att4 = jnp.concatenate(att4, axis=1).astype(BF16)
            if c == 1:
                c_wo.wait()
            for n in range(NT):
                pr_s[n * OWN : (n + 1) * OWN, :] = dot(att4, wo_s[:, n * WIDTH : (n + 1) * WIDTH])
            pr_send[c] = pr_s[...].astype(BF16)
            for i, peer in enumerate(y_peers):
                remote(pr_send.at[c], pr_recv.at[i], p_sem.at[2 * c], p_sem.at[1], (peer[0] - 1 + c, peer[1]))
            if c == 0:
                remote(pr_send.at[0], pr_recv.at[NT - 1], p_sem.at[0], p_sem.at[1], partner)
            else:
                pr_recv[NT - 1] = pr_send[1]

    @pl.when(core == 0)
    def _():
        c_wo.wait()

    for i, dx in enumerate((1, 3, 2)):
        compact(i + 1, dx)
    c_pg.wait()

    @pl.when(core == 0)
    def _():
        wait(pr_recv, p_sem.at[1])

    @pl.when(core == 1)
    def _():
        wait(pr_recv.at[pl.ds(0, NT - 1)], p_sem.at[1])

    whole = pr_recv[0].astype(F32) + pr_recv[1].astype(F32) + pr_recv[2].astype(F32) + pr_recv[3].astype(F32)
    pr_s[...] = whole
    quarters = [pr_s[n * OWN : (n + 1) * OWN, :] for n in range(NT)]
    squares = sum(part * part for part in quarters)
    power = jnp.sum(squares, axis=1, keepdims=True)
    own = quarters[0]
    for n in range(1, NT):
        own = jnp.where(tp == n, quarters[n], own)
    normed = own * lax.rsqrt(power / (NT * WIDTH) + EPS) * pg_s[...]
    residual = hid_s[:, pl.ds(pl.multiple_of(tp * WIDTH, WIDTH), WIDTH)].astype(F32)
    out_h[...] = (residual + normed).astype(BF16)

    wait(sq_recv.at[0], sq_sem.at[0])
    wait(sq_recv.at[1], sq_sem.at[2])
    @pl.when(core == 0)
    def _():
        wait(kfull.at[:, first_block, :], swap_sem.at[0])
        wait(vfull.at[:, first_block, :], swap_sem.at[2])
        wait(qbuf.at[pl.ds(0, NX * NZ)], q_send)

    @pl.when(core == 1)
    def _():
        wait(qbuf.at[pl.ds(0, NX * NZ - 1)], q_send)
        wait(sbuf.at[pl.ds(0, 2 * (NX * NZ - 1))], s_sem.at[0])
        wait(obuf.at[pl.ds(0, 2 * (NX * NZ - 1))], o_sem.at[0])
        wait(pr_recv, p_sem.at[0])
        wait(pr_recv.at[pl.ds(0, NT - 1)], p_sem.at[2])

    wait(kbuf.at[0, 0, pl.ds(0, NZ - 1)], z_sem.at[0])
    wait(vbuf.at[0, 0, pl.ds(0, NZ - 1)], z_sem.at[2])
    wait(kbuf.at[0, pl.ds(0, NX - 1)], x_sem.at[0])
    wait(vbuf.at[0, pl.ds(0, NX - 1)], x_sem.at[1])
    for i in range(NX):
        wait(kbuf.at[0, 0], c_sem.at[4 * i])
        wait(vbuf.at[0, 0], c_sem.at[4 * i + 2])


def hand_out(a, b, c, out_a, out_b, out_c, sem):
    copies = [
        pltpu.make_async_copy(src, dst, sem.at[i])
        for i, (src, dst) in enumerate(((b, out_b), (c, out_c), (a, out_a)))
    ]
    for copy in copies:
        copy.start()
    for copy in copies:
        copy.wait()


def body(hid, wq, wk, wv, wo, qg, kg, pg, kc, vc, lens, parents, leaf):
    half = np.arange(HEAD_DIM // 2, dtype=np.float32)
    freqs = np.power(np.float32(THETA), np.float32(-2.0) * half / np.float32(HEAD_DIM)).astype(np.float32)
    freq = jnp.asarray(np.concatenate([freqs, freqs])[None])
    vmem, sems = pltpu.VMEM, pltpu.SemaphoreType.DMA
    full = NC * BLOCK
    scratch = [
        vmem(hid.shape, BF16), vmem(wq.shape, BF16), vmem(wk.shape, BF16), vmem(wv.shape, BF16), vmem(wo.shape, BF16),
        vmem((1, WIDTH), F32), vmem((1, WIDTH), F32), vmem((1, WIDTH), F32),
        vmem(parents.shape, jnp.int32), vmem((1, HEAD_DIM), F32),
        pltpu.SMEM(lens.shape, jnp.int32), pltpu.SMEM(leaf.shape, jnp.int32),
        vmem((REQ, full, WIDTH), BF16), vmem((REQ, full, WIDTH), BF16), vmem((REQ, DRAFT, DRAFT), BF16),
        vmem((2, 8, HEAD_DIM), F32), vmem((2, NT - 1, 8, HEAD_DIM), F32),
        vmem((ROWS, HEAD_DIM), BF16), vmem((ROWS, HEAD_DIM), BF16), vmem((ROWS, HEAD_DIM), BF16),
        vmem((NC * NX * NZ, ROWS, HEAD_DIM), BF16),
        vmem((NC, NX, NZ, ROWS, HEAD_DIM), BF16), vmem((NC, NX, NZ, ROWS, HEAD_DIM), BF16),
        vmem((NC * NX, NZ, ROWS, HEAD_DIM), BF16), vmem((NC * NX, 1, 2 * HEAD_DIM), F32),
        vmem((NC * NX * NZ, ROWS, HEAD_DIM), BF16), vmem((NC * NX * NZ, 1, 2 * HEAD_DIM), F32),
        vmem((ROWS, HEAD_DIM), F32), vmem((ROWS, WIDTH), F32),
        vmem((NC, ROWS, WIDTH), BF16), vmem((NT, ROWS, WIDTH), BF16),
        sems((14,)), sems((4,)), sems((4,)), sems((NC * NX,)), sems, sems((4,)), sems((8,)), sems((16,)),
        sems((3,)), sems((3,)), sems((3,)), pltpu.SemaphoreType.REGULAR,
    ]
    anywhere = pl.BlockSpec(memory_space=pltpu.HBM)
    results = pl.pallas_call(
        kernel,
        out_shape=(vmem((OWN, WIDTH), BF16), vmem(kc.shape, BF16), vmem(vc.shape, BF16)),
        in_specs=[anywhere] * 14,
        out_specs=(pl.BlockSpec(memory_space=pltpu.VMEM),) * 3,
        scratch_shapes=scratch,
        compiler_params=pltpu.CompilerParams(
            collective_id=0, has_side_effects=True, vmem_limit_bytes=VMEM1
        ),
        cost_estimate=pl.CostEstimate(flops=300000000, bytes_accessed=11000000, transcendentals=200000),
        name="tree_attention",
    )(*(pltpu.with_memory_space_constraint(part, pltpu.HBM) for part in (
        hid, wq, wk, wv, wo, qg.reshape(1, WIDTH), kg.reshape(1, WIDTH), pg.reshape(1, WIDTH),
        kc, vc, lens, parents, leaf, freq,
    )))
    return pl.pallas_call(
        hand_out,
        out_shape=tuple(jax.ShapeDtypeStruct(part.shape, part.dtype) for part in results),
        in_specs=[pl.BlockSpec(memory_space=pltpu.VMEM)] * 3,
        out_specs=(anywhere,) * 3,
        scratch_shapes=[sems((3,))],
        compiler_params=pltpu.CompilerParams(vmem_limit_bytes=VMEM2),
        cost_estimate=pl.CostEstimate(flops=0, bytes_accessed=2200000, transcendentals=0),
        name="hand_out",
    )(*results)


def solution(mesh):
    return jax.shard_map(
        body,
        mesh=mesh,
        in_specs=(
            P("seq", None),
            P(None, "tp"),
            P(None, "tp"),
            P(None, "tp"),
            P("tp", None),
            P("tp"),
            P("tp"),
            P("tp"),
            P(None, "seq", "tp"),
            P(None, "seq", "tp"),
            P(),
            P(),
            P(),
        ),
        out_specs=(P("seq", "tp"), P(None, "seq", "tp"), P(None, "seq", "tp")),
        check_vma=False,
    )
```

```python
import math

import jax
import jax.numpy as jnp
import numpy as np
from jax import lax
from jax.experimental import pallas as pl
from jax.experimental.pallas import tpu as pltpu
from jax.sharding import PartitionSpec as P

HEAD_DIM = 128
EPS = 1e-06
THETA = 500000.0
NEG = -1e30
NX, NZ, NC, NT = 4, 8, 2, 4
HEADS = 4
OWN = 4
ROWS = HEADS * OWN
DRAFT = 64
REQ = 4
WIDTH = HEADS * HEAD_DIM
BLOCK = 128
MESH = pl.DeviceIdType.MESH
F32 = jnp.float32
BF16 = jnp.bfloat16
VMEM1 = 48 * 1024 * 1024
VMEM2 = 16 * 1024 * 1024
PLANES = (2, 1, 3, 0)
FAR_Z = (4, 3, 5, 2, 6, 1, 7, 0)


def far_first():
    hops = lambda a, b: min(a, NX - a) + min(b, NZ - b)
    pairs = [(a, b) for a in range(NX) for b in range(NZ) if (a, b) != (0, 0)]
    return sorted(pairs, key=lambda pair: -hops(*pair))


def iota(shape, dim):
    return lax.broadcasted_iota(jnp.int32, shape, dim)


def nt_dot(a, b):
    return lax.dot_general(a, b, (((1,), (1,)), ((), ())), preferred_element_type=F32)


def dot(a, b):
    return jnp.dot(a, b, preferred_element_type=F32)


def kernel(
    hid, wq, wk, wv, wo, qg, kg, pg, kc, vc, lens, par, leaf, freq,
    out_h, out_k, out_v,
    hid_s, wq_s, wk_s, wv_s, wo_s, qg_s, kg_s, pg_s, par_s, freq_s, lens_s, leaf_s,
    kfull, vfull, anc_s, sq_send, sq_recv, q_own, k_own, v_own, qbuf, kbuf, vbuf,
    o_st, s_st, obuf, sbuf, att_s, pr_s, pr_send, pr_recv,
    lsem, swap_sem, sq_sem, q_sem, q_send, z_sem, x_sem, c_sem, o_sem, s_sem, p_sem, plane_sem,
):
    seq = lax.axis_index("seq")
    tp = lax.axis_index("tp")
    core = lax.rem(seq, NC)
    zz = lax.rem(seq // NC, NZ)
    xx = seq // (NC * NZ)

    def at(dx, dz, on=core):
        return ((lax.rem(xx + dx, NX) * NZ + lax.rem(zz + dz, NZ)) * NC + on, tp)

    partner = (seq + 1 - 2 * core, tp)
    y_peers = [(seq, lax.rem(tp + d, NT)) for d in (2, 1, 3)]
    plane_peers = [at(a, b, 1) for a, b in far_first()]
    x_peers = [at(a, 0) for a in range(1, NX)]
    near_peers = [at(0, b) for b in range(1, NZ)] + x_peers + y_peers + [partner]

    barrier = pltpu.get_barrier_semaphore()
    for peer in near_peers:
        pl.semaphore_signal(barrier, inc=1, device_id=peer, device_id_type=MESH)

    @pl.when(core == 1)
    def _():
        for dz in range(1, NZ):
            pl.semaphore_signal(barrier, inc=1, device_id=at(0, dz, 0), device_id_type=MESH)

    pairs = [
        (par, par_s), (hid, hid_s), (wq, wq_s), (lens, lens_s), (freq, freq_s), (qg, qg_s), (kg, kg_s),
        (wk, wk_s), (wv, wv_s), (pg, pg_s), (leaf, leaf_s),
        (kc, kfull.at[:, pl.ds(core * BLOCK, BLOCK), :]),
        (vc, vfull.at[:, pl.ds(core * BLOCK, BLOCK), :]),
        (wo, wo_s),
    ]
    local = [pltpu.make_async_copy(a, b, lsem.at[i]) for i, (a, b) in enumerate(pairs)]
    for copy in local:
        copy.start()
    (c_par, c_hid, c_wq, c_lens, c_freq, c_qg, c_kg, c_wk, c_wv, c_pg, c_leaf, c_kc, c_vc, c_wo) = local

    def remote(src, dst, send, recv, peer):
        copy = pltpu.make_async_remote_copy(
            src_ref=src, dst_ref=dst, send_sem=send, recv_sem=recv, device_id=peer, device_id_type=MESH
        )
        copy.start()

    def wait(ref, sem):
        pltpu.make_async_copy(ref, ref, sem).wait()

    c_par.wait()
    square = (DRAFT, DRAFT)
    eye = (iota(square, 0) == iota(square, 1)).astype(F32)
    chains = []
    for r in range(REQ):
        up = (par_s[pl.ds(r, 1), :] == iota(square, 0)).astype(F32)
        chains.append((eye + up).astype(BF16))
    for _ in range(6):
        chains = [jnp.minimum(dot(a, a), 1.0).astype(BF16) for a in chains]
    for r in range(REQ):
        anc_s[r] = chains[r]

    chunk = (ROWS, HEAD_DIM)
    row_head = (iota(chunk, 0) >> 2) & 3
    lane = iota(chunk, 1)

    def ancestors_of(c):
        row_token = (zz * NC + c) * OWN + (iota((ROWS, DRAFT), 0) & 3)
        one_hot = (iota((ROWS, DRAFT), 1) == row_token).astype(F32).astype(BF16)
        return nt_dot(one_hot, anc_s[xx])

    anc_rows = ancestors_of(core)
    depth = jnp.sum(anc_rows, axis=1, keepdims=True) - 1.0
    c_lens.wait()
    position = lens_s[xx].astype(F32) + depth
    c_freq.wait()
    angle = position * freq_s[...]
    cosine = jnp.cos(angle)
    sine = jnp.sin(angle)
    sine = jnp.where(lane < HEAD_DIM // 2, -sine, sine)

    c_hid.wait()
    h4 = hid_s[...].astype(F32)
    h8 = jnp.concatenate([h4, h4], axis=0)
    h16 = jnp.concatenate([h8, h8], axis=0).astype(BF16)

    def diagonal(wide):
        picked = wide[:, :HEAD_DIM]
        for h in range(1, HEADS):
            picked = jnp.where(row_head == h, wide[:, h * HEAD_DIM : (h + 1) * HEAD_DIM], picked)
        return picked

    def spread(gain):
        return diagonal(jnp.broadcast_to(gain, (ROWS, WIDTH)))

    lane8 = iota((8, HEAD_DIM), 1)

    def turned(wide, gain):
        x = diagonal(wide) * spread(gain)
        return x * cosine + pltpu.roll(x, HEAD_DIM // 2, 1) * sine

    def square_sum(wide):
        return jnp.broadcast_to(jnp.sum(wide * wide, axis=1, keepdims=True)[:8], (8, HEAD_DIM))

    def scaled(x, i):
        wait(sq_recv.at[i], sq_sem.at[2 * i + 1])
        total = sq_send[i] + sq_recv[i, 0] + sq_recv[i, 1] + sq_recv[i, 2]
        scale = lax.rsqrt(total / (NT * WIDTH) + EPS)
        return (x * jnp.concatenate([scale, scale], axis=0)).astype(BF16)

    c_wq.wait()
    q_wide = dot(h16, wq_s[...])
    sq_send[0] = square_sum(q_wide)

    pl.semaphore_wait(barrier, len(near_peers) + (NZ - 1) * (1 - core))
    for i, peer in enumerate(y_peers):
        remote(sq_send.at[0], sq_recv.at[0, i], sq_sem.at[0], sq_sem.at[1], peer)
    for peer in x_peers:
        pl.semaphore_signal(plane_sem, inc=1, device_id=peer, device_id_type=MESH)

    for copy in (c_qg, c_kg):
        copy.wait()
    q_turn = turned(q_wide, qg_s[...])
    c_wk.wait()
    k_wide = dot(h16, wk_s[...])
    sq_send[1] = square_sum(k_wide)
    for i, peer in enumerate(y_peers):
        remote(sq_send.at[1], sq_recv.at[1, i], sq_sem.at[2], sq_sem.at[3], peer)
    mine = pl.ds(core * BLOCK, BLOCK)
    first_block = pl.ds(0, BLOCK)

    @pl.when(core == 0)
    def _():
        remote(kc, kfull.at[:, first_block, :], swap_sem.at[0], swap_sem.at[1], partner)
        remote(vc, vfull.at[:, first_block, :], swap_sem.at[2], swap_sem.at[3], partner)

    k_turn = turned(k_wide, kg_s[...])
    c_wv.wait()
    v_own[...] = diagonal(dot(h16, wv_s[...])).astype(BF16)
    for dz in FAR_Z[:-1]:
        remote(v_own, vbuf.at[core, xx, zz], z_sem.at[2], z_sem.at[3], at(0, dz))
    pltpu.make_async_copy(v_own, vbuf.at[core, xx, zz], z_sem.at[3]).start()

    q_own[...] = scaled(q_turn, 0)
    pl.semaphore_wait(plane_sem, len(x_peers))

    slot = xx * NZ + zz
    q_ready = q_sem.at[core * NX + xx]
    for peer in plane_peers:
        remote(q_own, qbuf.at[core * NX * NZ + slot], q_send, q_ready, peer)

    @pl.when(core == 0)
    def _():
        remote(q_own, qbuf.at[slot], q_send, q_ready, partner)

    @pl.when(core == 1)
    def _():
        pltpu.make_async_copy(q_own, qbuf.at[NX * NZ + slot], q_ready).start()

    k_own[...] = scaled(k_turn, 1)
    for dz in FAR_Z[:-1]:
        remote(k_own, kbuf.at[core, xx, zz], z_sem.at[0], z_sem.at[1], at(0, dz))
    pltpu.make_async_copy(k_own, kbuf.at[core, xx, zz], z_sem.at[1]).start()

    def onward(buf, sem, first, at_x, at_c):
        wait(buf.at[core, xx], z_sem.at[sem])
        for far in (2, 1, 3):
            remote(buf.at[core, xx], buf.at[core, xx], x_sem.at[first], x_sem.at[at_x + far], at(far, 0))
        remote(buf.at[core, xx], buf.at[core, xx], c_sem.at[at_c], c_sem.at[at_c + 1], partner)

    factor = 1.0 / math.sqrt(HEAD_DIM)
    c_kc.wait()
    c_vc.wait()

    @pl.when(core == 0)
    def _():
        onward(vbuf, 3, 1, 4, 2)
        onward(kbuf, 1, 0, 1, 0)

    @pl.when(core == 1)
    def _():
        tall = (NZ * ROWS, NC * BLOCK)
        tall_head = (iota(tall, 0) >> 2) & 3
        place = (seq - 1) * BLOCK + iota(tall, 1)
        half_rows = NZ * ROWS // 2
        half_shape = (half_rows, HEAD_DIM)
        peak_spot = iota(half_shape, 1) == iota(half_shape, 0)
        sum_spot = iota(half_shape, 1) == iota(half_shape, 0) + half_rows
        onward(vbuf, 3, 1, 4, 2)
        wait(kfull.at[:, first_block, :], swap_sem.at[1])
        wait(vfull.at[:, first_block, :], swap_sem.at[3])
        for step, (c, dx) in enumerate([(1, 0), (1, 1), (1, 3), (1, 2), (0, 2), (0, 1), (0, 3), (0, 0)]):
            if step == 3:
                onward(kbuf, 1, 0, 1, 0)
            r = lax.rem(xx + dx, NX)
            group = pl.ds((c * NX + r) * NZ, NZ)
            wait(qbuf.at[group], q_sem.at[c * NX + r])
            queries = qbuf[group].reshape(NZ * ROWS, HEAD_DIM)
            scores = None
            for h in range(HEADS):
                part = nt_dot(queries, kfull[r, :, h * HEAD_DIM : (h + 1) * HEAD_DIM])
                scores = part if h == 0 else jnp.where(tall_head == h, part, scores)
            visible = place < lens_s[r]
            scores = jnp.where(visible, scores * factor, NEG)
            peak = jnp.max(scores, axis=1, keepdims=True)
            weights = jnp.where(visible, jnp.exp(scores - peak), 0.0)
            weight_sum = jnp.sum(weights, axis=1, keepdims=True)
            mixed = None
            for h in range(HEADS):
                masked = jnp.where(tall_head == h, weights, 0.0).astype(BF16)
                part = dot(masked, vfull[r, :, h * HEAD_DIM : (h + 1) * HEAD_DIM])
                mixed = part if h == 0 else mixed + part
            o_st[step] = mixed.astype(BF16).reshape(NZ, ROWS, HEAD_DIM)
            for n in range(2):
                rows = slice(n * half_rows, (n + 1) * half_rows)
                spots = jnp.where(peak_spot, peak[rows], jnp.where(sum_spot, weight_sum[rows], 0.0))
                s_st[step, n] = jnp.sum(spots, axis=0, keepdims=True)
            there = c * NX * NZ + slot
            for dz in FAR_Z:
                to = lax.rem(zz + dz, NZ)
                if (dx, dz) == (0, 0):
                    pltpu.make_async_copy(o_st.at[step, to], obuf.at[there], o_sem.at[1 + c]).start()
                    pltpu.make_async_copy(s_st.at[step, to // (NZ // 2)], sbuf.at[there], s_sem.at[1 + c]).start()
                else:
                    remote(s_st.at[step, to // (NZ // 2)], sbuf.at[there], s_sem.at[0], s_sem.at[1 + c], at(dx, dz))
                    remote(o_st.at[step, to], obuf.at[there], o_sem.at[0], o_sem.at[1 + c], at(dx, dz))

    wait(kbuf.at[core, xx], c_sem.at[1])
    wait(vbuf.at[core, xx], c_sem.at[3])
    both = NC * NZ * ROWS
    col = iota((DRAFT, both), 1)
    col_token = ((col >> 4) & 7) * (NC * OWN) + (col >> 7) * OWN + (col & 3)
    expand = (iota((DRAFT, both), 0) == col_token).astype(F32).astype(BF16)

    def request_rows(buf, r):
        return jnp.concatenate([buf[c, r].reshape(NZ * ROWS, HEAD_DIM) for c in range(NC)], axis=0)

    for i, dx in enumerate((1, 3, 2)):
        r = lax.rem(xx + dx, NX)
        wait(kbuf.at[core, r], x_sem.at[1 + (NX - dx)])
        wait(vbuf.at[core, r], x_sem.at[4 + (NX - dx)])
        remote(kbuf.at[core, r], kbuf.at[core, r], c_sem.at[4 + 4 * i], c_sem.at[5 + 4 * i], partner)
        remote(vbuf.at[core, r], vbuf.at[core, r], c_sem.at[6 + 4 * i], c_sem.at[7 + 4 * i], partner)

    c_leaf.wait()
    p_place = (seq * BLOCK + iota((BLOCK, DRAFT), 0)).astype(F32)
    col_head = (iota((BLOCK, both), 1) >> 2) & 3

    def compact(i, dx):
        r = lax.rem(xx + dx, NX)
        if dx:
            wait(kbuf.at[core, r], c_sem.at[1 + 4 * i])
            wait(vbuf.at[core, r], c_sem.at[3 + 4 * i])
        anc = anc_s[r]
        target = jnp.sum(anc.astype(F32), axis=0, keepdims=True) - 1.0 + lens_s[r].astype(F32)
        leaf_hot = (iota((ROWS, DRAFT), 1) == leaf_s[r]).astype(F32).astype(BF16)
        on_path = nt_dot(leaf_hot, anc)[:1]
        placing = jnp.where((p_place == target) & (on_path > 0.5), 1.0, 0.0)
        written = jnp.sum(placing, axis=1, keepdims=True) > 0.5
        placing = dot(placing.astype(BF16), expand)
        k_rows = request_rows(kbuf, r)
        v_rows = request_rows(vbuf, r)
        for h in range(HEADS):
            columns = slice(h * HEAD_DIM, (h + 1) * HEAD_DIM)
            pick = jnp.where(col_head == h, placing, 0.0).astype(BF16)
            old_k = kfull[r, mine, columns].astype(F32)
            old_v = vfull[r, mine, columns].astype(F32)
            out_k[r, :, columns] = jnp.where(written, dot(pick, k_rows), old_k).astype(BF16)
            out_v[r, :, columns] = jnp.where(written, dot(pick, v_rows), old_v).astype(BF16)

    compact(0, 0)

    @pl.when(core == 1)
    def _():
        wide_shape = (ROWS, both)
        same_head = ((iota(wide_shape, 1) >> 2) & 3) == ((iota(wide_shape, 0) >> 2) & 3)
        here = lane == lax.rem(zz, NZ // 2) * ROWS + iota(chunk, 0)

        def column(row):
            return jnp.sum(jnp.where(here, row, 0.0), axis=1, keepdims=True)

        drafts = []
        for c in (1, 0):
            allowed = (dot(ancestors_of(c).astype(BF16), expand) > 0.5) & same_head
            d_scores = nt_dot(qbuf[c * NX * NZ + slot], request_rows(kbuf, xx)) * factor
            d_scores = jnp.where(allowed, d_scores, NEG)
            d_peak = jnp.max(d_scores, axis=1, keepdims=True)
            d_weights = jnp.where(allowed, jnp.exp(d_scores - d_peak), 0.0)
            d_sum = jnp.sum(d_weights, axis=1, keepdims=True)
            drafts.append((c, d_peak, d_sum, dot(d_weights.astype(BF16), request_rows(vbuf, xx))))
        for c, d_peak, d_sum, d_out in drafts:
            base = c * NX * NZ
            arrived = pl.ds(base, NX * NZ)
            wait(sbuf.at[arrived], s_sem.at[1 + c])
            wait(obuf.at[arrived], o_sem.at[1 + c])
            stats = sbuf[arrived]
            highest = jnp.max(stats, axis=0)
            shares = jnp.exp(stats - highest[None])
            sums = shares[0] * pltpu.roll(stats[0], HEAD_DIM // 2, 1)
            for s in range(1, NX * NZ):
                sums = sums + shares[s] * pltpu.roll(stats[s], HEAD_DIM // 2, 1)
            top = column(highest)
            merged = None
            for s in range(NX * NZ):
                part = column(shares[s]) * obuf[base + s].astype(F32)
                merged = part if s == 0 else merged + part
            best = jnp.maximum(top, d_peak)
            c_share = jnp.exp(top - best)
            d_share = jnp.exp(d_peak - best)
            att_s[...] = (merged * c_share + d_out * d_share) / (column(sums) * c_share + d_sum * d_share)
            att4 = [att_s[h * OWN : (h + 1) * OWN, :] for h in range(HEADS)]
            att4 = jnp.concatenate(att4, axis=1).astype(BF16)
            if c == 1:
                c_wo.wait()
            for n in range(NT):
                pr_s[n * OWN : (n + 1) * OWN, :] = dot(att4, wo_s[:, n * WIDTH : (n + 1) * WIDTH])
            pr_send[c] = pr_s[...].astype(BF16)
            for i, peer in enumerate(y_peers):
                remote(pr_send.at[c], pr_recv.at[i], p_sem.at[2 * c], p_sem.at[1], (peer[0] - 1 + c, peer[1]))
            if c == 0:
                remote(pr_send.at[0], pr_recv.at[NT - 1], p_sem.at[0], p_sem.at[1], partner)
            else:
                pr_recv[NT - 1] = pr_send[1]

    @pl.when(core == 0)
    def _():
        c_wo.wait()

    for i, dx in enumerate((1, 3, 2)):
        compact(i + 1, dx)
    c_pg.wait()

    @pl.when(core == 0)
    def _():
        wait(pr_recv, p_sem.at[1])

    @pl.when(core == 1)
    def _():
        wait(pr_recv.at[pl.ds(0, NT - 1)], p_sem.at[1])

    whole = pr_recv[0].astype(F32) + pr_recv[1].astype(F32) + pr_recv[2].astype(F32) + pr_recv[3].astype(F32)
    pr_s[...] = whole
    quarters = [pr_s[n * OWN : (n + 1) * OWN, :] for n in range(NT)]
    squares = sum(part * part for part in quarters)
    power = jnp.sum(squares, axis=1, keepdims=True)
    own = quarters[0]
    for n in range(1, NT):
        own = jnp.where(tp == n, quarters[n], own)
    normed = own * lax.rsqrt(power / (NT * WIDTH) + EPS) * pg_s[...]
    residual = hid_s[:, pl.ds(pl.multiple_of(tp * WIDTH, WIDTH), WIDTH)].astype(F32)
    out_h[...] = (residual + normed).astype(BF16)

    wait(sq_recv.at[0], sq_sem.at[0])
    wait(sq_recv.at[1], sq_sem.at[2])
    @pl.when(core == 0)
    def _():
        wait(kfull.at[:, first_block, :], swap_sem.at[0])
        wait(vfull.at[:, first_block, :], swap_sem.at[2])
        wait(qbuf.at[pl.ds(0, NX * NZ)], q_send)

    @pl.when(core == 1)
    def _():
        wait(qbuf.at[pl.ds(0, NX * NZ - 1)], q_send)
        wait(sbuf.at[pl.ds(0, 2 * (NX * NZ - 1))], s_sem.at[0])
        wait(obuf.at[pl.ds(0, 2 * (NX * NZ - 1))], o_sem.at[0])
        wait(pr_recv, p_sem.at[0])
        wait(pr_recv.at[pl.ds(0, NT - 1)], p_sem.at[2])

    wait(kbuf.at[0, 0, pl.ds(0, NZ - 1)], z_sem.at[0])
    wait(vbuf.at[0, 0, pl.ds(0, NZ - 1)], z_sem.at[2])
    wait(kbuf.at[0, pl.ds(0, NX - 1)], x_sem.at[0])
    wait(vbuf.at[0, pl.ds(0, NX - 1)], x_sem.at[1])
    for i in range(NX):
        wait(kbuf.at[0, 0], c_sem.at[4 * i])
        wait(vbuf.at[0, 0], c_sem.at[4 * i + 2])


def hand_out(a, b, c, out_a, out_b, out_c, sem):
    copies = [
        pltpu.make_async_copy(src, dst, sem.at[i])
        for i, (src, dst) in enumerate(((b, out_b), (c, out_c), (a, out_a)))
    ]
    for copy in copies:
        copy.start()
    for copy in copies:
        copy.wait()


def body(hid, wq, wk, wv, wo, qg, kg, pg, kc, vc, lens, parents, leaf):
    half = np.arange(HEAD_DIM // 2, dtype=np.float32)
    freqs = np.power(np.float32(THETA), np.float32(-2.0) * half / np.float32(HEAD_DIM)).astype(np.float32)
    freq = jnp.asarray(np.concatenate([freqs, freqs])[None])
    vmem, sems = pltpu.VMEM, pltpu.SemaphoreType.DMA
    full = NC * BLOCK
    scratch = [
        vmem(hid.shape, BF16), vmem(wq.shape, BF16), vmem(wk.shape, BF16), vmem(wv.shape, BF16), vmem(wo.shape, BF16),
        vmem((1, WIDTH), F32), vmem((1, WIDTH), F32), vmem((1, WIDTH), F32),
        vmem(parents.shape, jnp.int32), vmem((1, HEAD_DIM), F32),
        pltpu.SMEM(lens.shape, jnp.int32), pltpu.SMEM(leaf.shape, jnp.int32),
        vmem((REQ, full, WIDTH), BF16), vmem((REQ, full, WIDTH), BF16), vmem((REQ, DRAFT, DRAFT), BF16),
        vmem((2, 8, HEAD_DIM), F32), vmem((2, NT - 1, 8, HEAD_DIM), F32),
        vmem((ROWS, HEAD_DIM), BF16), vmem((ROWS, HEAD_DIM), BF16), vmem((ROWS, HEAD_DIM), BF16),
        vmem((NC * NX * NZ, ROWS, HEAD_DIM), BF16),
        vmem((NC, NX, NZ, ROWS, HEAD_DIM), BF16), vmem((NC, NX, NZ, ROWS, HEAD_DIM), BF16),
        vmem((NC * NX, NZ, ROWS, HEAD_DIM), BF16), vmem((NC * NX, 2, 1, HEAD_DIM), F32),
        vmem((NC * NX * NZ, ROWS, HEAD_DIM), BF16), vmem((NC * NX * NZ, 1, HEAD_DIM), F32),
        vmem((ROWS, HEAD_DIM), F32), vmem((ROWS, WIDTH), F32),
        vmem((NC, ROWS, WIDTH), BF16), vmem((NT, ROWS, WIDTH), BF16),
        sems((14,)), sems((4,)), sems((4,)), sems((NC * NX,)), sems, sems((4,)), sems((8,)), sems((16,)),
        sems((3,)), sems((3,)), sems((3,)), pltpu.SemaphoreType.REGULAR,
    ]
    anywhere = pl.BlockSpec(memory_space=pltpu.HBM)
    results = pl.pallas_call(
        kernel,
        out_shape=(vmem((OWN, WIDTH), BF16), vmem(kc.shape, BF16), vmem(vc.shape, BF16)),
        in_specs=[anywhere] * 14,
        out_specs=(pl.BlockSpec(memory_space=pltpu.VMEM),) * 3,
        scratch_shapes=scratch,
        compiler_params=pltpu.CompilerParams(
            collective_id=0, has_side_effects=True, vmem_limit_bytes=VMEM1
        ),
        cost_estimate=pl.CostEstimate(flops=300000000, bytes_accessed=11000000, transcendentals=200000),
        name="tree_attention",
    )(*(pltpu.with_memory_space_constraint(part, pltpu.HBM) for part in (
        hid, wq, wk, wv, wo, qg.reshape(1, WIDTH), kg.reshape(1, WIDTH), pg.reshape(1, WIDTH),
        kc, vc, lens, parents, leaf, freq,
    )))
    return pl.pallas_call(
        hand_out,
        out_shape=tuple(jax.ShapeDtypeStruct(part.shape, part.dtype) for part in results),
        in_specs=[pl.BlockSpec(memory_space=pltpu.VMEM)] * 3,
        out_specs=(anywhere,) * 3,
        scratch_shapes=[sems((3,))],
        compiler_params=pltpu.CompilerParams(vmem_limit_bytes=VMEM2),
        cost_estimate=pl.CostEstimate(flops=0, bytes_accessed=2200000, transcendentals=0),
        name="hand_out",
    )(*results)


def solution(mesh):
    return jax.shard_map(
        body,
        mesh=mesh,
        in_specs=(
            P("seq", None),
            P(None, "tp"),
            P(None, "tp"),
            P(None, "tp"),
            P("tp", None),
            P("tp"),
            P("tp"),
            P("tp"),
            P(None, "seq", "tp"),
            P(None, "seq", "tp"),
            P(),
            P(),
            P(),
        ),
        out_specs=(P("seq", "tp"), P(None, "seq", "tp"), P(None, "seq", "tp")),
        check_vma=False,
    )
```
